32 devices in a mesh: det: 8 (over z, y), tm: 4 (over x, core).
Axes of the slice: x: 2, y: 2, z: 4, core: 2. Of those that a mesh axis runs over, the one named last changes fastest.
Arguments:
- timestreams: float32 [2048, 24000], P('det', 'tm'), may hold values from -6 to 6
- wafer_group: int32 [2048], P('det'), may hold values from 0 to 11
- valid_blocks: int32 [2048, 200], P('det', 'tm'), may hold values 0 or 1
- gain_guess: float32 [2048], P('det'), may hold values from 0.5 to 2
- inverse_psd: float32 [12, 24000], replicated, may hold values from 0.05 to 1
Outputs:
- filtered: float32 [2048, 24000], P('det', 'tm')
- gains: float32 [2048], P('det')
- template: float32 [12, 24000], P(None, 'tm')
The draws below stay inside these ranges and needn't reach their ends.
All inputs are finite; a program needn't handle non-finite values. No bound on the sum of `valid_blocks` on one device may be relied on, other than what follows from the above.
Results may differ from the reference program's by a relative error of at most 0.00027.
Values sent between devices are 32-bit elements; how exact they have to be, the bound alone decides.
A program may use at most 128 MiB of HBM per device.

```python
import math
import jax
import jax.numpy as jnp
from jax import lax

DET_DEV = 256
G = 12
FLAG_BLOCK = 120
ITERS = 3
NDET = 2048
NSAMP = 24000
NBLK = 200
N_DET = 8


def set_ends(entries, stream_key, low, largest):
    longest = entries.shape.index(max(entries.shape))
    spots = []
    for shift in (0, 1):
        where = [jax.random.randint(jax.random.fold_in(stream_key, axis), (), 0, length) for axis, length in enumerate(entries.shape)]
        where[longest] = (where[longest] + shift) % entries.shape[longest]
        spots.append(tuple(where))
    return entries.at[spots[0]].set(low).at[spots[1]].set(largest)


def level_of(rng, extent, cuts, smallest, largest):
    def one(position, blocks):
        heights = jax.random.uniform(jax.random.fold_in(jax.random.fold_in(rng, 6), position), (blocks,), jnp.float32, smallest / len(cuts), largest / len(cuts))
        return jnp.repeat(jnp.exp(heights), extent[position] // blocks).reshape((-1,) + (1,) * (len(extent) - position - 1))

    factor_of = one(*cuts[0])
    for cut in cuts[1:]:
        factor_of = factor_of * one(*cut)
    return factor_of


def bell_draw(own_key, extent, deviation, limit, split=(), kind=jnp.bfloat16):
    gain = level_of(own_key, extent, split, -0.22, 0.18) if split else 1.0
    entries = jax.random.normal(own_key, extent, jnp.float32) * deviation * gain
    return jnp.minimum(jnp.maximum(entries, -limit), limit).astype(kind)


def setup_inputs(seed: int = 0) -> dict:
    keys = jax.random.split(jax.random.key(seed), 6)
    timestreams = bell_draw(keys[0], (NDET, NSAMP), 1.0, 6.0, ((0, 8), (1, 4)), jnp.float32)
    wafer_group = set_ends(jax.random.randint(keys[1], (NDET,), 0, G), jax.random.fold_in(keys[1], 1), 0, G - 1).astype(jnp.int32)
    valid_blocks = set_ends((jax.random.randint(keys[2], (NDET, NBLK), 0, 8) < 7).astype(jnp.int32), jax.random.fold_in(keys[2], 1), 0, 1)
    gain_guess = jnp.clip(jnp.exp(math.log(2.0) - 1.3862944 * jax.random.uniform(keys[3], (NDET,), jnp.float32) ** level_of(keys[3], (NDET,), ((0, 8),), -0.2, 0.2)), 0.5, 2.0)
    inverse_psd = jnp.clip(jnp.exp(jax.random.uniform(keys[4], (G, NSAMP), jnp.float32, math.log(0.05), math.log(1.0))), 0.05, 1.0)
    return {"timestreams": timestreams, "wafer_group": wafer_group, "valid_blocks": valid_blocks, "gain_guess": gain_guess, "inverse_psd": inverse_psd}


def filter_block(pair):
    cleaned, groups = pair
    spectrum = jnp.fft.fft(cleaned, axis=1) * jnp.take(inverse_psd_table[0], groups, axis=0)
    return jnp.real(jnp.fft.ifft(spectrum, axis=1))
inverse_psd_table = [None]

def reference(timestreams, wafer_group, valid_blocks, gain_guess, inverse_psd):
    highest = lax.Precision.HIGHEST
    mask = jnp.repeat(valid_blocks.astype(jnp.float32), FLAG_BLOCK, axis=1)
    onehot = (wafer_group[:, None] == jnp.arange(G, dtype=jnp.int32)[None, :]).astype(jnp.float32)
    counts = lax.optimization_barrier(jnp.sum(onehot, axis=0))
    masked = mask * timestreams
    gains = gain_guess
    template = jnp.zeros((G, NSAMP), jnp.float32)
    per_det = jnp.zeros_like(masked)
    for rounds in range(ITERS):
        squares = jnp.dot(gains * gains, onehot, precision=highest)
        scale = jnp.sqrt(squares / jnp.maximum(counts, 1.0) + 1e-05)
        normed = gains / jnp.dot(onehot, scale, precision=highest)
        sum_one = jnp.dot(onehot.T, masked * normed[:, None], precision=highest)
        sum_two = jnp.dot(onehot.T, mask * (normed * normed)[:, None], precision=highest)
        template = sum_one / (1.0 + sum_two)
        per_det = jnp.dot(onehot, template, precision=highest)
        numer = lax.optimization_barrier(jnp.sum(masked * per_det, axis=1))
        denom = lax.optimization_barrier(jnp.sum(mask * per_det * per_det, axis=1))
        gains = numer / (1.0 + denom)
    cleaned = masked - gains[:, None] * mask * per_det
    weights = inverse_psd

    def one_block(pair):
        rows, groups = pair
        spectrum = jnp.fft.fft(rows, axis=1) * jnp.take(weights, groups, axis=0)
        return jnp.real(jnp.fft.ifft(spectrum, axis=1)).astype(cleaned.dtype)
    filtered = lax.map(one_block, (cleaned.reshape(N_DET, DET_DEV, NSAMP), wafer_group.reshape(N_DET, DET_DEV)))
    return (filtered.reshape(NDET, NSAMP), gains, template)
```

```python
import functools
import math

import jax
import jax.numpy as jnp
import numpy as np
from jax import lax
from jax.experimental import pallas as pl
from jax.experimental.pallas import tpu as pltpu
from jax.sharding import PartitionSpec as P

ITERS = 3
Q = 250
QP = 256
GP = 16
CHUNK = 8
MESH = pl.DeviceIdType.MESH
F32 = jnp.float32
BF16 = jnp.bfloat16
NT_DIMS = (((1,), (1,)), ((), ()))


def dot(a, b):
    return jnp.dot(a, b, preferred_element_type=F32)


def dot_nt(a, b):
    return lax.dot_general(a, b, NT_DIMS, preferred_element_type=F32)


def split(a):
    hi = a.astype(BF16)
    return hi, (a - hi.astype(F32)).astype(BF16)


def np_split(a):
    hi = a.astype(BF16)
    return hi, (a - hi.astype(np.float64)).astype(BF16)


def fit_kernel(nd, nt, slabs, own, cyc, rows,
               x_hbm, v_ref, vrc_ref, group_ref, guess_ref, e_ref,
               raw_ref, vraw_ref, tmpl_ref, gains_ref,
               xv, xh, xl, part, small, rbuf, rsmall, tbuf, red,
               load_sem, loc_sem, raw_s, raw_r, val_s, val_r, ps, pr, ss, sr, ts, tr, gs, gr, fs, fr):
    det = lax.axis_index("det")
    tm = lax.axis_index("tm")
    cycles = slabs // cyc
    share = rows // nt * slabs
    vshare = rows // nt * cycles

    def det_peer(off):
        return lax.rem(det + off, nd)

    def tm_peer(off):
        return lax.rem(tm + off, nt)

    loads = [pltpu.make_async_copy(x_hbm.at[:, pl.ds(128 * h, 128)], xv.at[h], load_sem.at[h])
             for h in range(QP // 128)]
    for load in loads:
        load.start()
    barrier = pltpu.get_barrier_semaphore()
    for off in range(1, nd):
        pl.semaphore_signal(barrier, inc=1, device_id=(det_peer(off), tm), device_id_type=MESH)
    for off in range(1, nt):
        pl.semaphore_signal(barrier, inc=1, device_id=(det, tm_peer(off)), device_id_type=MESH)
    pl.semaphore_wait(barrier, nd + nt - 2)

    waits = []
    for off in range(1, nt):
        peer = tm_peer(off)
        copy = pltpu.make_async_remote_copy(
            src_ref=x_hbm.at[pl.ds(peer * share, share)], dst_ref=raw_ref.at[tm],
            send_sem=raw_s.at[off], recv_sem=raw_r.at[off],
            device_id=(det, peer), device_id_type=MESH)
        copy.start()
        waits.append(copy)
        copy = pltpu.make_async_remote_copy(
            src_ref=vrc_ref.at[pl.ds(peer * vshare, vshare)], dst_ref=vraw_ref.at[tm],
            send_sem=val_s.at[off], recv_sem=val_r.at[off],
            device_id=(det, peer), device_id_type=MESH)
        copy.start()
        waits.append(copy)
    own_raw = pltpu.make_async_copy(x_hbm.at[pl.ds(tm * share, share)], raw_ref.at[tm], loc_sem.at[1])
    own_raw.start()
    own_val = pltpu.make_async_copy(vrc_ref.at[pl.ds(tm * vshare, vshare)], vraw_ref.at[tm], loc_sem.at[2])
    own_val.start()
    for load in loads:
        load.wait()

    def prepare(i, carry):
        spread = e_ref[i]
        for c in range(cycles):
            slab = c * cyc + i
            mask = dot(v_ref[c], spread)
            x = jnp.concatenate(
                [xv[h, pl.ds(slab, rows, stride=slabs), :] for h in range(QP // 128)], axis=1)
            hi, lo = split(mask * x)
            xh[slab] = hi
            xl[slab] = lo
        return carry

    lax.fori_loop(0, cyc, prepare, 0)

    hot = (lax.broadcasted_iota(jnp.int32, (GP, rows), 0) == group_ref[...]).astype(F32)
    lane = lax.broadcasted_iota(jnp.int32, (GP, 128), 1)
    gains = guess_ref[...]
    padded = own * nd
    for it in range(ITERS):
        weight = hot * gains
        wh, wl = split(weight)
        wboth = jnp.concatenate([wh, wl], axis=0)
        power = hot * (gains * gains)
        ph, plo = split(power)
        squares = jnp.sum(power, axis=1, keepdims=True)
        counts = jnp.sum(hot, axis=1, keepdims=True)
        for c in range(cycles):
            block_sum = dot(ph, v_ref[c]) + dot(plo, v_ref[c])
            small[it, c] = jnp.where(lane == 64, squares, jnp.where(lane == 65, counts, block_sum))

        copies = []
        for off in range(1, nd):
            copy = pltpu.make_async_remote_copy(
                src_ref=small.at[it], dst_ref=rsmall.at[it, off],
                send_sem=ss.at[it, off], recv_sem=sr.at[it, off],
                device_id=(det_peer(off), tm), device_id_type=MESH)
            copy.start()
            copies.append(copy)

        def weigh(owner):
            def one(k, carry):
                slab = jnp.minimum(owner * own + k, slabs - 1)
                both = dot(wboth, xh[slab])
                part[it, owner * own + k] = both[:GP] + both[GP:] + dot(wh, xl[slab])
                return carry
            lax.fori_loop(0, own, one, 0, unroll=True)

        for off in range(1, nd):
            peer = det_peer(off)
            weigh(peer)
            copy = pltpu.make_async_remote_copy(
                src_ref=part.at[it, pl.ds(peer * own, own)], dst_ref=rbuf.at[it, off],
                send_sem=ps.at[it, off], recv_sem=pr.at[it, off],
                device_id=(peer, tm), device_id_type=MESH)
            copy.start()
            copies.append(copy)
        weigh(det)
        for copy in copies:
            copy.wait_recv()
        waits_send = copies

        first = small[it]
        for off in range(1, nd):
            first = first + rsmall[it, off]
        scale = jnp.sqrt(first[0][:, 64:65] / jnp.maximum(first[0][:, 65:66], 1.0) + 1e-05)
        small[ITERS] = first
        for k in range(own):
            slab = det * own + k
            total = part[it, slab]
            for off in range(1, nd):
                total = total + rbuf[it, off, k]
            safe = jnp.minimum(slab, slabs - 1)
            sums = small[ITERS, lax.div(safe, cyc)]
            sums = jnp.where(lane < 64, sums, 0.0)
            s1, s2 = split(sums)
            spread = e_ref[lax.rem(safe, cyc)]
            wide = dot(s1, spread) + dot(s2, spread)
            tbuf[it, slab] = (total / scale) / (1.0 + wide / (scale * scale))
        gather = []
        for off in range(1, nd):
            copy = pltpu.make_async_remote_copy(
                src_ref=tbuf.at[it, pl.ds(det * own, own)], dst_ref=tbuf.at[it, pl.ds(det * own, own)],
                send_sem=ts.at[it, off], recv_sem=tr.at[it, off],
                device_id=(det_peer(off), tm), device_id_type=MESH)
            copy.start()
            gather.append(copy)
        for off in range(1, nd):
            source = lax.rem(det + nd - off, nd)
            pltpu.make_async_remote_copy(
                src_ref=tbuf.at[it, pl.ds(source * own, own)], dst_ref=tbuf.at[it, pl.ds(source * own, own)],
                send_sem=ts.at[it, off], recv_sem=tr.at[it, off],
                device_id=(det_peer(off), tm), device_id_type=MESH).wait_recv()
        waits_send = waits_send + gather

        if it == ITERS - 1:
            for off in range(1, nt):
                copy = pltpu.make_async_remote_copy(
                    src_ref=tbuf.at[it, pl.ds(0, slabs)], dst_ref=tmpl_ref.at[tm],
                    send_sem=fs.at[off], recv_sem=fr.at[off],
                    device_id=(det, tm_peer(off)), device_id_type=MESH)
                copy.start()
                waits.append(copy)
            own_tmpl = pltpu.make_async_copy(tbuf.at[it, pl.ds(0, slabs)], tmpl_ref.at[tm], loc_sem.at[3])
            own_tmpl.start()

        def correlate(i, carry):
            inner, blocks = carry
            new_blocks = []
            for c in range(cycles):
                slab = c * cyc + i
                th, tl = split(tbuf[it, slab])
                both = dot_nt(jnp.concatenate([th, tl], axis=0), xh[slab])
                inner = inner + both[:GP] + both[GP:] + dot_nt(th, xl[slab])
                sh, sl = split(tbuf[it, slab] * tbuf[it, slab])
                both = dot_nt(jnp.concatenate([sh, sl], axis=0), e_ref[i])
                new_blocks.append(blocks[c] + both[:GP] + both[GP:])
            return inner, tuple(new_blocks)

        inner, blocks = lax.fori_loop(
            0, cyc, correlate,
            (jnp.zeros((GP, rows), F32), tuple(jnp.zeros((GP, 128), F32) for _ in range(cycles))))
        norm = jnp.zeros((GP, rows), F32)
        for c in range(cycles):
            bh, bl = split(blocks[c])
            norm = norm + dot_nt(bh, v_ref[c]) + dot_nt(bl, v_ref[c])
        numer = jnp.sum(hot * inner, axis=0, keepdims=True)
        denom = jnp.sum(hot * norm, axis=0, keepdims=True)
        red[it, tm] = jnp.concatenate([numer, denom, jnp.zeros((6, rows), F32)], axis=0)
        copies = []
        for off in range(1, nt):
            copy = pltpu.make_async_remote_copy(
                src_ref=red.at[it, tm], dst_ref=red.at[it, tm],
                send_sem=gs.at[it, off], recv_sem=gr.at[it, off],
                device_id=(det, tm_peer(off)), device_id_type=MESH)
            copy.start()
            copies.append(copy)
        for off in range(1, nt):
            source = lax.rem(tm + nt - off, nt)
            pltpu.make_async_remote_copy(
                src_ref=red.at[it, source], dst_ref=red.at[it, source],
                send_sem=gs.at[it, off], recv_sem=gr.at[it, off],
                device_id=(det, tm_peer(off)), device_id_type=MESH).wait_recv()
        total = red[it, 0]
        for t in range(1, nt):
            total = total + red[it, t]
        gains = total[0:1] / (1.0 + total[1:2])
        for copy in waits_send + copies:
            copy.wait_send()

    gains_ref[...] = gains
    own_raw.wait()
    own_val.wait()
    own_tmpl.wait()
    for copy in waits:
        copy.wait()


def filter_kernel(nt, slabs, cyc, count, half,
                  group_ref, gain_ref, raw_ref, v_ref, tmpl_ref, w_ref, e_ref,
                  f1_ref, tw_ref, m2_ref, m3_ref, f4_ref,
                  out_ref, mask, stage, spec, ybuf, loc_sem, send, recv):
    det = lax.axis_index("det")
    tm = lax.axis_index("tm")
    total = slabs * nt
    span = CHUNK * slabs
    chunks = count // CHUNK
    cycles = slabs // cyc

    barrier = pltpu.get_barrier_semaphore()
    for off in range(1, nt):
        pl.semaphore_signal(barrier, inc=1, device_id=(det, lax.rem(tm + off, nt)), device_id_type=MESH)
    pl.semaphore_wait(barrier, nt - 1)

    def spread(i, carry):
        for t in range(nt):
            wide = dot(v_ref[t].astype(BF16), e_ref[i])
            for h in range(QP // 128):
                mask[t, h, pl.ds(i, count * cycles, stride=cyc), :] = wide[:, 128 * h:128 * (h + 1)]
        return carry

    lax.fori_loop(0, cyc, spread, 0)

    def remote(chunk, off):
        peer = lax.rem(tm + off, nt)
        return pltpu.make_async_remote_copy(
            src_ref=ybuf.at[peer, pl.ds(chunk * span, span)],
            dst_ref=out_ref.at[pl.ds((tm * chunks + chunk) * span, span)],
            send_sem=send.at[chunk, off], recv_sem=recv.at[chunk, off],
            device_id=(det, peer), device_id_type=MESH)

    def local(chunk):
        return pltpu.make_async_copy(
            ybuf.at[tm, pl.ds(chunk * span, span)],
            out_ref.at[pl.ds((tm * chunks + chunk) * span, span)], loc_sem.at[chunk])

    def three(a, b):
        hi, lo = split(a)
        return dot(hi, b[0]) + dot(lo, b[0]) + dot(hi, b[1])

    def rows_of(read, chunk, k):
        if slabs % 8 == 0:
            return read(pl.ds((chunk * CHUNK + k) * slabs, slabs))
        return read(pl.ds(chunk * span, span))[k * slabs:(k + 1) * slabs]

    def work(chunk, carry):
        for k in range(CHUNK):
            row = chunk * CHUNK + k
            g = group_ref[row]
            parts = []
            for t in range(nt):
                seen = jnp.concatenate(
                    [rows_of(lambda at: mask[t, h, at, :], chunk, k) for h in range(QP // 128)], axis=1)
                stream = rows_of(lambda at: raw_ref[t, at, :], chunk, k)
                parts.append(seen * (stream - gain_ref[row] * tmpl_ref[g, pl.ds(t * slabs, slabs), :]))
            x = jnp.concatenate(parts, axis=0)
            hi, lo = split(x)
            both = dot(f1_ref[...], hi)
            y = both[:2 * half] + both[2 * half:] + dot(f1_ref[pl.ds(0, 2 * half), :], lo)
            re, im = y[:half], y[half:]
            stage[pl.ds(k * half, half), pl.ds(0, QP)] = re * tw_ref[0] + im * tw_ref[1]
            stage[pl.ds(k * half, half), pl.ds(QP, QP)] = im * tw_ref[0] - re * tw_ref[1]
        spec[...] = three(stage[...], m2_ref)
        for k in range(CHUNK):
            w = w_ref[group_ref[chunk * CHUNK + k]]
            for h in range(2):
                at = (pl.ds(k * half, half), pl.ds(h * QP, QP))
                spec[at] = spec[at] * w
        stage[...] = three(spec[...], m3_ref)
        held = []
        for k in range(CHUNK):
            row = chunk * CHUNK + k
            re = stage[pl.ds(k * half, half), pl.ds(0, QP)]
            im = stage[pl.ds(k * half, half), pl.ds(QP, QP)]
            v = jnp.concatenate([re * tw_ref[0] - im * tw_ref[1], im * tw_ref[0] + re * tw_ref[1]], axis=0)
            hi, lo = split(v)
            both = dot(f4_ref[...], hi)
            y = both[:total] + both[total:] + dot(f4_ref[pl.ds(0, total), :], lo)
            held.append(y)
            if slabs % 8 == 0:
                for t in range(nt):
                    ybuf[t, pl.ds(row * slabs, slabs), :] = y[t * slabs:(t + 1) * slabs]
        if slabs % 8:
            for t in range(nt):
                ybuf[t, pl.ds(chunk * span, span), :] = jnp.concatenate(
                    [y[t * slabs:(t + 1) * slabs] for y in held], axis=0)
        for off in range(1, nt):
            remote(chunk, off).start()
        local(chunk).start()
        return carry

    lax.fori_loop(0, chunks, work, 0)

    def finish(chunk, carry):
        local(chunk).wait()
        for off in range(1, nt):
            remote(chunk, off).wait_send()
        for off in range(1, nt):
            source = lax.rem(tm + nt - off, nt)
            pltpu.make_async_remote_copy(
                src_ref=ybuf.at[source, pl.ds(chunk * span, span)],
                dst_ref=out_ref.at[pl.ds((source * chunks + chunk) * span, span)],
                send_sem=send.at[chunk, off], recv_sem=recv.at[chunk, off],
                device_id=(det, source), device_id_type=MESH).wait_recv()
        return carry

    lax.fori_loop(0, chunks, finish, 0)


def constants(total):
    length = total * Q
    half = -(-(total // 2 + 1) // 8) * 8
    kp = np.arange(total // 2 + 1)
    n = kp.size
    p = np.arange(total)
    angle = 2 * np.pi / total * (kp[:, None] * p[None, :] % total)
    f1 = np.zeros((2 * half, total))
    f1[:n] = np.cos(angle)
    f1[half:half + n] = -np.sin(angle)
    hi, lo = np_split(f1)
    f1 = np.concatenate([hi, lo], axis=0)
    twice = np.where((kp == 0) | (2 * kp == total), 1.0, 2.0) / length
    f4 = np.zeros((total, 2 * half))
    f4[:, :n] = (np.cos(angle) * twice[:, None]).T
    f4[:, half:half + n] = -(np.sin(angle) * twice[:, None]).T
    hi, lo = np_split(f4)
    f4 = np.concatenate([hi, lo], axis=0)
    q = np.arange(Q)
    angle = 2 * np.pi / length * (kp[:, None] * q[None, :])
    tw = np.zeros((2, half, QP), np.float32)
    tw[0, :n, :Q] = np.cos(angle)
    tw[1, :n, :Q] = np.sin(angle)
    angle = 2 * np.pi / Q * (q[:, None] * q[None, :] % Q)
    c, s = np.cos(angle), np.sin(angle)

    def complex_table(sign):
        m = np.zeros((2 * QP, 2 * QP))
        m[:Q, :Q] = c
        m[QP:QP + Q, :Q] = -sign * s
        m[:Q, QP:QP + Q] = sign * s
        m[QP:QP + Q, QP:QP + Q] = c
        return np.stack(np_split(m))

    return half, n, f1, f4, tw, complex_table(-1.0), complex_table(1.0)


def local(timestreams, wafer_group, valid_blocks, gain_guess, inverse_psd):
    nd, nt = lax.axis_size("det"), lax.axis_size("tm")
    rows, samp = timestreams.shape
    groups = inverse_psd.shape[0]
    block = samp // valid_blocks.shape[1]
    cyc = block // math.gcd(block, Q)
    per = cyc * Q // block
    slabs = samp // Q
    cycles = slabs // cyc
    own = -(-slabs // nd)
    padded = own * nd
    count = rows // nt
    total = slabs * nt
    half, n, f1, f4, tw, m2, m3 = constants(total)
    spread = np.zeros((cyc, 128, QP), np.float32)
    for i in range(cyc):
        spread[i, (i * Q + np.arange(Q)) // block, np.arange(Q)] = 1.0
    e = jnp.asarray(spread.astype(BF16))

    x2 = jnp.pad(timestreams.reshape(rows, slabs, Q), ((0, 0), (0, 0), (0, QP - Q))).reshape(rows * slabs, QP)
    vrc = jnp.pad(valid_blocks.astype(F32).reshape(rows, cycles, per), ((0, 0), (0, 0), (0, 128 - per)))
    v = jnp.transpose(vrc, (1, 0, 2)).astype(BF16)
    vrc = vrc.reshape(rows * cycles, 128)

    vmem = pl.BlockSpec(memory_space=pltpu.VMEM)
    hbm = pl.BlockSpec(memory_space=pl.ANY)
    smem = pl.BlockSpec(memory_space=pltpu.SMEM)
    dma = pltpu.SemaphoreType.DMA
    raw, vraw, tmpl, gains = pl.pallas_call(
        functools.partial(fit_kernel, nd, nt, slabs, own, cyc, rows),
        out_shape=(
            jax.ShapeDtypeStruct((nt, count * slabs, QP), F32),
            jax.ShapeDtypeStruct((nt, count * cycles, 128), F32),
            jax.ShapeDtypeStruct((nt, slabs, GP, QP), F32),
            jax.ShapeDtypeStruct((1, rows), F32),
        ),
        in_specs=[hbm, vmem, vmem, vmem, vmem, vmem],
        out_specs=(hbm, vmem, hbm, vmem),
        scratch_shapes=[
            pltpu.VMEM((QP // 128, rows * slabs, 128), F32),
            pltpu.VMEM((slabs, rows, QP), BF16),
            pltpu.VMEM((slabs, rows, QP), BF16),
            pltpu.VMEM((ITERS, padded, GP, QP), F32),
            pltpu.VMEM((ITERS + 1, cycles, GP, 128), F32),
            pltpu.VMEM((ITERS, nd, own, GP, QP), F32),
            pltpu.VMEM((ITERS, nd, cycles, GP, 128), F32),
            pltpu.VMEM((ITERS, padded, GP, QP), F32),
            pltpu.VMEM((ITERS, nt, 8, rows), F32),
            dma((QP // 128,)), dma((4,)), dma((nt,)), dma((nt,)), dma((nt,)), dma((nt,)),
            dma((ITERS, nd)), dma((ITERS, nd)), dma((ITERS, nd)), dma((ITERS, nd)),
            dma((ITERS, nd)), dma((ITERS, nd)), dma((ITERS, nt)), dma((ITERS, nt)),
            dma((nt,)), dma((nt,)),
        ],
        compiler_params=pltpu.CompilerParams(
            collective_id=0, has_side_effects=True, vmem_limit_bytes=50 * 2**20),
        name="fit",
    )(x2, v, vrc, wafer_group.reshape(1, rows), gain_guess.reshape(1, rows), e)

    gains = gains.reshape(rows)
    mine = lax.axis_index("tm")
    template = lax.dynamic_index_in_dim(tmpl, mine, 0, False)[:, :groups, :Q]
    template = jnp.transpose(template, (1, 0, 2)).reshape(groups, samp)
    by_group = jnp.transpose(tmpl.reshape(total, GP, QP), (1, 0, 2))[:groups]
    even = 0.5 * (inverse_psd + jnp.roll(jnp.flip(inverse_psd, 1), 1, axis=1))
    weights = jnp.transpose(even.reshape(groups, Q, total)[:, :, :n], (0, 2, 1))
    weights = jnp.pad(weights, ((0, 0), (0, half - n), (0, QP - Q)))
    my_group = lax.dynamic_slice_in_dim(wafer_group, mine * count, count)
    my_gains = lax.dynamic_slice_in_dim(gains, mine * count, count)

    out = pl.pallas_call(
        functools.partial(filter_kernel, nt, slabs, cyc, count, half),
        out_shape=jax.ShapeDtypeStruct((rows * slabs, QP), F32),
        in_specs=[smem, smem] + [vmem] * 10,
        out_specs=hbm,
        scratch_shapes=[
            pltpu.VMEM((nt, QP // 128, count * slabs, 128), F32),
            pltpu.VMEM((CHUNK * half, 2 * QP), F32),
            pltpu.VMEM((CHUNK * half, 2 * QP), F32),
            pltpu.VMEM((nt, count * slabs, QP), F32),
            dma((count // CHUNK,)), dma((count // CHUNK, nt)), dma((count // CHUNK, nt)),
        ],
        compiler_params=pltpu.CompilerParams(
            collective_id=1, has_side_effects=True, vmem_limit_bytes=50 * 2**20),
        name="filter",
    )(my_group, my_gains, raw, vraw, by_group, weights, e,
      jnp.asarray(f1), jnp.asarray(tw), jnp.asarray(m2), jnp.asarray(m3), jnp.asarray(f4))
    filtered = out.reshape(rows, slabs, QP)[:, :, :Q].reshape(rows, samp)
    return (filtered, gains, template)


def solution(mesh):
    in_specs = (P("det", "tm"), P("det"), P("det", "tm"), P("det"), P())
    out_specs = (P("det", "tm"), P("det"), P(None, "tm"))
    return jax.shard_map(local, mesh=mesh, in_specs=in_specs, out_specs=out_specs, check_vma=False)
```

```python
import functools
import math

import jax
import jax.numpy as jnp
import numpy as np
from jax import lax
from jax.experimental import pallas as pl
from jax.experimental.pallas import tpu as pltpu
from jax.sharding import PartitionSpec as P

ITERS = 3
Q = 250
QP = 256
GP = 16
HALVES = QP // 128
BAND = 32
CHUNK = 8
MESH = pl.DeviceIdType.MESH
F32 = jnp.float32
BF16 = jnp.bfloat16
NT_DIMS = (((1,), (1,)), ((), ()))


def dot(a, b):
    return jnp.dot(a, b, preferred_element_type=F32)


def dot_nt(a, b):
    return lax.dot_general(a, b, NT_DIMS, preferred_element_type=F32)


def split(a):
    hi = a.astype(BF16)
    return hi, (a - hi.astype(F32)).astype(BF16)


def np_split(a):
    hi = a.astype(BF16)
    return hi, (a - hi.astype(np.float64)).astype(BF16)


def pack_kernel(slabs, x_ref, out_ref):
    for p in range(slabs):
        wide = x_ref[:, Q * p:Q * (p + 1)]
        wide = jnp.concatenate([wide, jnp.zeros((BAND, QP - Q), F32)], axis=1)
        for h in range(HALVES):
            out_ref[h, pl.ds(p, BAND, stride=slabs), :] = wide[:, 128 * h:128 * (h + 1)]


def unpack_kernel(slabs, y_ref, out_ref):
    for p in range(slabs):
        wide = jnp.concatenate([y_ref[h, pl.ds(p, BAND, stride=slabs), :] for h in range(HALVES)], axis=1)
        out_ref[:, Q * p:Q * (p + 1)] = wide[:, :Q]


def fit_kernel(nd, nt, slabs, own, cyc, rows,
               x_hbm, v_ref, vrc_ref, group_ref, guess_ref, e_ref,
               raw_ref, vraw_ref, tmpl_ref, gains_ref,
               xv, xh, xl, part, small, rbuf, rsmall, tbuf, red,
               loc_sem, raw_s, raw_r, val_s, val_r, ps, pr, ss, sr, ts, tr, gs, gr, fs, fr):
    det = lax.axis_index("det")
    tm = lax.axis_index("tm")
    cycles = slabs // cyc
    share = rows // nt * slabs
    vshare = rows // nt * cycles

    def det_peer(off):
        return lax.rem(det + off, nd)

    def tm_peer(off):
        return lax.rem(tm + off, nt)

    load = pltpu.make_async_copy(x_hbm, xv, loc_sem.at[0])
    load.start()
    barrier = pltpu.get_barrier_semaphore()
    for off in range(1, nd):
        pl.semaphore_signal(barrier, inc=1, device_id=(det_peer(off), tm), device_id_type=MESH)
    for off in range(1, nt):
        pl.semaphore_signal(barrier, inc=1, device_id=(det, tm_peer(off)), device_id_type=MESH)
    pl.semaphore_wait(barrier, nd + nt - 2)

    waits = []
    for off in range(1, nt):
        peer = tm_peer(off)
        copy = pltpu.make_async_remote_copy(
            src_ref=x_hbm.at[:, pl.ds(peer * share, share)], dst_ref=raw_ref.at[tm],
            send_sem=raw_s.at[off], recv_sem=raw_r.at[off],
            device_id=(det, peer), device_id_type=MESH)
        copy.start()
        waits.append(copy)
        copy = pltpu.make_async_remote_copy(
            src_ref=vrc_ref.at[pl.ds(peer * vshare, vshare)], dst_ref=vraw_ref.at[tm],
            send_sem=val_s.at[off], recv_sem=val_r.at[off],
            device_id=(det, peer), device_id_type=MESH)
        copy.start()
        waits.append(copy)
    own_raw = pltpu.make_async_copy(x_hbm.at[:, pl.ds(tm * share, share)], raw_ref.at[tm], loc_sem.at[1])
    own_raw.start()
    own_val = pltpu.make_async_copy(vrc_ref.at[pl.ds(tm * vshare, vshare)], vraw_ref.at[tm], loc_sem.at[2])
    own_val.start()
    load.wait()

    def prepare(i, carry):
        spread = e_ref[i]
        for c in range(cycles):
            slab = c * cyc + i
            mask = dot(v_ref[c], spread)
            x = jnp.concatenate(
                [xv[h, pl.ds(slab, rows, stride=slabs), :] for h in range(HALVES)], axis=1)
            hi, lo = split(mask * x)
            xh[slab] = hi
            xl[slab] = lo
        return carry

    lax.fori_loop(0, cyc, prepare, 0)

    hot = (lax.broadcasted_iota(jnp.int32, (GP, rows), 0) == group_ref[...]).astype(F32)
    lane = lax.broadcasted_iota(jnp.int32, (GP, 128), 1)
    gains = guess_ref[...]
    padded = own * nd
    for it in range(ITERS):
        weight = hot * gains
        wh, wl = split(weight)
        wboth = jnp.concatenate([wh, wl], axis=0)
        power = hot * (gains * gains)
        ph, plo = split(power)
        squares = jnp.sum(power, axis=1, keepdims=True)
        counts = jnp.sum(hot, axis=1, keepdims=True)
        for c in range(cycles):
            block_sum = dot(ph, v_ref[c]) + dot(plo, v_ref[c])
            small[it, c] = jnp.where(lane == 64, squares, jnp.where(lane == 65, counts, block_sum))

        copies = []
        for off in range(1, nd):
            copy = pltpu.make_async_remote_copy(
                src_ref=small.at[it], dst_ref=rsmall.at[it, off],
                send_sem=ss.at[it, off], recv_sem=sr.at[it, off],
                device_id=(det_peer(off), tm), device_id_type=MESH)
            copy.start()
            copies.append(copy)

        def weigh(owner):
            def one(k, carry):
                slab = jnp.minimum(owner * own + k, slabs - 1)
                both = dot(wboth, xh[slab])
                part[it, owner * own + k] = both[:GP] + both[GP:] + dot(wh, xl[slab])
                return carry
            lax.fori_loop(0, own, one, 0, unroll=True)

        for off in range(1, nd):
            peer = det_peer(off)
            weigh(peer)
            copy = pltpu.make_async_remote_copy(
                src_ref=part.at[it, pl.ds(peer * own, own)], dst_ref=rbuf.at[it, off],
                send_sem=ps.at[it, off], recv_sem=pr.at[it, off],
                device_id=(peer, tm), device_id_type=MESH)
            copy.start()
            copies.append(copy)
        weigh(det)
        for copy in copies:
            copy.wait_recv()
        waits_send = copies

        first = small[it]
        for off in range(1, nd):
            first = first + rsmall[it, off]
        scale = jnp.sqrt(first[0][:, 64:65] / jnp.maximum(first[0][:, 65:66], 1.0) + 1e-05)
        small[ITERS] = first
        for k in range(own):
            slab = det * own + k
            total = part[it, slab]
            for off in range(1, nd):
                total = total + rbuf[it, off, k]
            safe = jnp.minimum(slab, slabs - 1)
            sums = small[ITERS, lax.div(safe, cyc)]
            sums = jnp.where(lane < 64, sums, 0.0)
            s1, s2 = split(sums)
            spread = e_ref[lax.rem(safe, cyc)]
            wide = dot(s1, spread) + dot(s2, spread)
            tbuf[it, slab] = (total / scale) / (1.0 + wide / (scale * scale))
        gather = []
        for off in range(1, nd):
            copy = pltpu.make_async_remote_copy(
                src_ref=tbuf.at[it, pl.ds(det * own, own)], dst_ref=tbuf.at[it, pl.ds(det * own, own)],
                send_sem=ts.at[it, off], recv_sem=tr.at[it, off],
                device_id=(det_peer(off), tm), device_id_type=MESH)
            copy.start()
            gather.append(copy)
        for off in range(1, nd):
            source = lax.rem(det + nd - off, nd)
            pltpu.make_async_remote_copy(
                src_ref=tbuf.at[it, pl.ds(source * own, own)], dst_ref=tbuf.at[it, pl.ds(source * own, own)],
                send_sem=ts.at[it, off], recv_sem=tr.at[it, off],
                device_id=(det_peer(off), tm), device_id_type=MESH).wait_recv()
        waits_send = waits_send + gather

        if it == ITERS - 1:
            for off in range(1, nt):
                copy = pltpu.make_async_remote_copy(
                    src_ref=tbuf.at[it, pl.ds(0, slabs)], dst_ref=tmpl_ref.at[tm],
                    send_sem=fs.at[off], recv_sem=fr.at[off],
                    device_id=(det, tm_peer(off)), device_id_type=MESH)
                copy.start()
                waits.append(copy)
            own_tmpl = pltpu.make_async_copy(tbuf.at[it, pl.ds(0, slabs)], tmpl_ref.at[tm], loc_sem.at[3])
            own_tmpl.start()

        def correlate(i, carry):
            inner, blocks = carry
            new_blocks = []
            for c in range(cycles):
                slab = c * cyc + i
                th, tl = split(tbuf[it, slab])
                both = dot_nt(jnp.concatenate([th, tl], axis=0), xh[slab])
                inner = inner + both[:GP] + both[GP:] + dot_nt(th, xl[slab])
                sh, sl = split(tbuf[it, slab] * tbuf[it, slab])
                both = dot_nt(jnp.concatenate([sh, sl], axis=0), e_ref[i])
                new_blocks.append(blocks[c] + both[:GP] + both[GP:])
            return inner, tuple(new_blocks)

        inner, blocks = lax.fori_loop(
            0, cyc, correlate,
            (jnp.zeros((GP, rows), F32), tuple(jnp.zeros((GP, 128), F32) for _ in range(cycles))))
        norm = jnp.zeros((GP, rows), F32)
        for c in range(cycles):
            bh, bl = split(blocks[c])
            norm = norm + dot_nt(bh, v_ref[c]) + dot_nt(bl, v_ref[c])
        numer = jnp.sum(hot * inner, axis=0, keepdims=True)
        denom = jnp.sum(hot * norm, axis=0, keepdims=True)
        red[it, tm] = jnp.concatenate([numer, denom, jnp.zeros((6, rows), F32)], axis=0)
        copies = []
        for off in range(1, nt):
            copy = pltpu.make_async_remote_copy(
                src_ref=red.at[it, tm], dst_ref=red.at[it, tm],
                send_sem=gs.at[it, off], recv_sem=gr.at[it, off],
                device_id=(det, tm_peer(off)), device_id_type=MESH)
            copy.start()
            copies.append(copy)
        for off in range(1, nt):
            source = lax.rem(tm + nt - off, nt)
            pltpu.make_async_remote_copy(
                src_ref=red.at[it, source], dst_ref=red.at[it, source],
                send_sem=gs.at[it, off], recv_sem=gr.at[it, off],
                device_id=(det, tm_peer(off)), device_id_type=MESH).wait_recv()
        total = red[it, 0]
        for t in range(1, nt):
            total = total + red[it, t]
        gains = total[0:1] / (1.0 + total[1:2])
        for copy in waits_send + copies:
            copy.wait_send()

    gains_ref[...] = gains
    own_raw.wait()
    own_val.wait()
    own_tmpl.wait()
    for copy in waits:
        copy.wait()


def filter_kernel(nt, slabs, cyc, count, half,
                  group_ref, gain_ref, raw_ref, v_ref, tmpl_ref, w_ref, e_ref,
                  f1_ref, tw_ref, m2_ref, m3_ref, f4_ref,
                  out_ref, mask, stage, spec, ybuf, loc_sem, send, recv):
    det = lax.axis_index("det")
    tm = lax.axis_index("tm")
    total = slabs * nt
    span = CHUNK * slabs
    chunks = count // CHUNK
    cycles = slabs // cyc

    barrier = pltpu.get_barrier_semaphore()
    for off in range(1, nt):
        pl.semaphore_signal(barrier, inc=1, device_id=(det, lax.rem(tm + off, nt)), device_id_type=MESH)
    pl.semaphore_wait(barrier, nt - 1)

    def spread(i, carry):
        for t in range(nt):
            wide = dot(v_ref[t].astype(BF16), e_ref[i])
            for h in range(HALVES):
                mask[t, h, pl.ds(i, count * cycles, stride=cyc), :] = wide[:, 128 * h:128 * (h + 1)]
        return carry

    lax.fori_loop(0, cyc, spread, 0)

    def remote(chunk, off):
        peer = lax.rem(tm + off, nt)
        return pltpu.make_async_remote_copy(
            src_ref=ybuf.at[peer, :, pl.ds(chunk * span, span)],
            dst_ref=out_ref.at[:, pl.ds((tm * chunks + chunk) * span, span)],
            send_sem=send.at[chunk, off], recv_sem=recv.at[chunk, off],
            device_id=(det, peer), device_id_type=MESH)

    def local(chunk):
        return pltpu.make_async_copy(
            ybuf.at[tm, :, pl.ds(chunk * span, span)],
            out_ref.at[:, pl.ds((tm * chunks + chunk) * span, span)], loc_sem.at[chunk])

    def three(a, b):
        hi, lo = split(a)
        return dot(hi, b[0]) + dot(lo, b[0]) + dot(hi, b[1])

    def rows_of(read, chunk, k):
        if slabs % 8 == 0:
            return read(pl.ds((chunk * CHUNK + k) * slabs, slabs))
        return read(pl.ds(chunk * span, span))[k * slabs:(k + 1) * slabs]

    def work(chunk, carry):
        for k in range(CHUNK):
            row = chunk * CHUNK + k
            g = group_ref[row]
            parts = []
            for t in range(nt):
                seen = jnp.concatenate(
                    [rows_of(lambda at: mask[t, h, at, :], chunk, k) for h in range(HALVES)], axis=1)
                stream = jnp.concatenate(
                    [rows_of(lambda at: raw_ref[t, h, at, :], chunk, k) for h in range(HALVES)], axis=1)
                parts.append(seen * (stream - gain_ref[row] * tmpl_ref[g, pl.ds(t * slabs, slabs), :]))
            x = jnp.concatenate(parts, axis=0)
            hi, lo = split(x)
            both = dot(f1_ref[...], hi)
            y = both[:2 * half] + both[2 * half:] + dot(f1_ref[pl.ds(0, 2 * half), :], lo)
            re, im = y[:half], y[half:]
            stage[pl.ds(k * half, half), pl.ds(0, QP)] = re * tw_ref[0] + im * tw_ref[1]
            stage[pl.ds(k * half, half), pl.ds(QP, QP)] = im * tw_ref[0] - re * tw_ref[1]
        spec[...] = three(stage[...], m2_ref)
        for k in range(CHUNK):
            w = w_ref[group_ref[chunk * CHUNK + k]]
            for h in range(2):
                at = (pl.ds(k * half, half), pl.ds(h * QP, QP))
                spec[at] = spec[at] * w
        stage[...] = three(spec[...], m3_ref)
        held = []
        for k in range(CHUNK):
            row = chunk * CHUNK + k
            re = stage[pl.ds(k * half, half), pl.ds(0, QP)]
            im = stage[pl.ds(k * half, half), pl.ds(QP, QP)]
            v = jnp.concatenate([re * tw_ref[0] - im * tw_ref[1], im * tw_ref[0] + re * tw_ref[1]], axis=0)
            hi, lo = split(v)
            both = dot(f4_ref[...], hi)
            y = both[:total] + both[total:] + dot(f4_ref[pl.ds(0, total), :], lo)
            held.append(y)
            if slabs % 8 == 0:
                for t in range(nt):
                    for h in range(HALVES):
                        ybuf[t, h, pl.ds(row * slabs, slabs), :] = y[t * slabs:(t + 1) * slabs, 128 * h:128 * (h + 1)]
        if slabs % 8:
            for t in range(nt):
                joined = jnp.concatenate([y[t * slabs:(t + 1) * slabs] for y in held], axis=0)
                for h in range(HALVES):
                    ybuf[t, h, pl.ds(chunk * span, span), :] = joined[:, 128 * h:128 * (h + 1)]
        for off in range(1, nt):
            remote(chunk, off).start()
        local(chunk).start()
        return carry

    lax.fori_loop(0, chunks, work, 0)

    def finish(chunk, carry):
        local(chunk).wait()
        for off in range(1, nt):
            remote(chunk, off).wait_send()
        for off in range(1, nt):
            source = lax.rem(tm + nt - off, nt)
            pltpu.make_async_remote_copy(
                src_ref=ybuf.at[source, :, pl.ds(chunk * span, span)],
                dst_ref=out_ref.at[:, pl.ds((source * chunks + chunk) * span, span)],
                send_sem=send.at[chunk, off], recv_sem=recv.at[chunk, off],
                device_id=(det, source), device_id_type=MESH).wait_recv()
        return carry

    lax.fori_loop(0, chunks, finish, 0)


def constants(total):
    length = total * Q
    half = -(-(total // 2 + 1) // 8) * 8
    kp = np.arange(total // 2 + 1)
    n = kp.size
    p = np.arange(total)
    angle = 2 * np.pi / total * (kp[:, None] * p[None, :] % total)
    f1 = np.zeros((2 * half, total))
    f1[:n] = np.cos(angle)
    f1[half:half + n] = -np.sin(angle)
    hi, lo = np_split(f1)
    f1 = np.concatenate([hi, lo], axis=0)
    twice = np.where((kp == 0) | (2 * kp == total), 1.0, 2.0) / length
    f4 = np.zeros((total, 2 * half))
    f4[:, :n] = (np.cos(angle) * twice[:, None]).T
    f4[:, half:half + n] = -(np.sin(angle) * twice[:, None]).T
    hi, lo = np_split(f4)
    f4 = np.concatenate([hi, lo], axis=0)
    q = np.arange(Q)
    angle = 2 * np.pi / length * (kp[:, None] * q[None, :])
    tw = np.zeros((2, half, QP), np.float32)
    tw[0, :n, :Q] = np.cos(angle)
    tw[1, :n, :Q] = np.sin(angle)
    angle = 2 * np.pi / Q * (q[:, None] * q[None, :] % Q)
    c, s = np.cos(angle), np.sin(angle)

    def complex_table(sign):
        m = np.zeros((2 * QP, 2 * QP))
        m[:Q, :Q] = c
        m[QP:QP + Q, :Q] = -sign * s
        m[:Q, QP:QP + Q] = sign * s
        m[QP:QP + Q, QP:QP + Q] = c
        return np.stack(np_split(m))

    return half, n, f1, f4, tw, complex_table(-1.0), complex_table(1.0)


def local(timestreams, wafer_group, valid_blocks, gain_guess, inverse_psd):
    nd, nt = lax.axis_size("det"), lax.axis_size("tm")
    rows, samp = timestreams.shape
    groups = inverse_psd.shape[0]
    block = samp // valid_blocks.shape[1]
    cyc = block // math.gcd(block, Q)
    per = cyc * Q // block
    slabs = samp // Q
    cycles = slabs // cyc
    own = -(-slabs // nd)
    padded = own * nd
    count = rows // nt
    total = slabs * nt
    half, n, f1, f4, tw, m2, m3 = constants(total)
    spread = np.zeros((cyc, 128, QP), np.float32)
    for i in range(cyc):
        spread[i, (i * Q + np.arange(Q)) // block, np.arange(Q)] = 1.0
    e = jnp.asarray(spread.astype(BF16))

    x2 = pl.pallas_call(
        functools.partial(pack_kernel, slabs),
        out_shape=jax.ShapeDtypeStruct((HALVES, rows * slabs, 128), F32),
        grid=(rows // BAND,),
        in_specs=[pl.BlockSpec((BAND, samp), lambda i: (i, 0))],
        out_specs=pl.BlockSpec((HALVES, BAND * slabs, 128), lambda i: (0, i, 0)),
        compiler_params=pltpu.CompilerParams(vmem_limit_bytes=32 * 2**20),
        name="pack",
    )(timestreams)
    vrc = jnp.pad(valid_blocks.astype(F32).reshape(rows, cycles, per), ((0, 0), (0, 0), (0, 128 - per)))
    v = jnp.transpose(vrc, (1, 0, 2)).astype(BF16)
    vrc = vrc.reshape(rows * cycles, 128)

    vmem = pl.BlockSpec(memory_space=pltpu.VMEM)
    hbm = pl.BlockSpec(memory_space=pl.ANY)
    smem = pl.BlockSpec(memory_space=pltpu.SMEM)
    dma = pltpu.SemaphoreType.DMA
    raw, vraw, tmpl, gains = pl.pallas_call(
        functools.partial(fit_kernel, nd, nt, slabs, own, cyc, rows),
        out_shape=(
            jax.ShapeDtypeStruct((nt, HALVES, count * slabs, 128), F32),
            jax.ShapeDtypeStruct((nt, count * cycles, 128), F32),
            jax.ShapeDtypeStruct((nt, slabs, GP, QP), F32),
            jax.ShapeDtypeStruct((1, rows), F32),
        ),
        in_specs=[hbm, vmem, vmem, vmem, vmem, vmem],
        out_specs=(hbm, vmem, hbm, vmem),
        scratch_shapes=[
            pltpu.VMEM((HALVES, rows * slabs, 128), F32),
            pltpu.VMEM((slabs, rows, QP), BF16),
            pltpu.VMEM((slabs, rows, QP), BF16),
            pltpu.VMEM((ITERS, padded, GP, QP), F32),
            pltpu.VMEM((ITERS + 1, cycles, GP, 128), F32),
            pltpu.VMEM((ITERS, nd, own, GP, QP), F32),
            pltpu.VMEM((ITERS, nd, cycles, GP, 128), F32),
            pltpu.VMEM((ITERS, padded, GP, QP), F32),
            pltpu.VMEM((ITERS, nt, 8, rows), F32),
            dma((4,)), dma((nt,)), dma((nt,)), dma((nt,)), dma((nt,)),
            dma((ITERS, nd)), dma((ITERS, nd)), dma((ITERS, nd)), dma((ITERS, nd)),
            dma((ITERS, nd)), dma((ITERS, nd)), dma((ITERS, nt)), dma((ITERS, nt)),
            dma((nt,)), dma((nt,)),
        ],
        compiler_params=pltpu.CompilerParams(
            collective_id=0, has_side_effects=True, vmem_limit_bytes=50 * 2**20),
        name="fit",
    )(x2, v, vrc, wafer_group.reshape(1, rows), gain_guess.reshape(1, rows), e)

    gains = gains.reshape(rows)
    mine = lax.axis_index("tm")
    template = lax.dynamic_index_in_dim(tmpl, mine, 0, False)[:, :groups, :Q]
    template = jnp.transpose(template, (1, 0, 2)).reshape(groups, samp)
    by_group = jnp.transpose(tmpl.reshape(total, GP, QP), (1, 0, 2))[:groups]
    kp = np.arange(n)
    pick = np.zeros((total, 2 * half), np.float32)
    pick[kp, kp] = 0.5
    pick[(total - kp) % total, half + kp] = 0.5
    both = jnp.einsum("gjp,pk->gkj", inverse_psd.reshape(groups, Q, total), pick, precision=lax.Precision.HIGHEST)
    flips = np.zeros((2, Q, QP), np.float32)
    flips[0, (Q - np.arange(Q)) % Q, np.arange(Q)] = 1.0
    flips[1, Q - 1 - np.arange(Q), np.arange(Q)] = 1.0
    edge = jnp.dot(both[:, half], flips[0], precision=lax.Precision.HIGHEST)
    inside = jnp.einsum("gkj,jq->gkq", both[:, half + 1:], flips[1], precision=lax.Precision.HIGHEST)
    weights = jnp.pad(both[:, :half], ((0, 0), (0, 0), (0, QP - Q))) + jnp.concatenate([edge[:, None], inside], axis=1)
    my_group = lax.dynamic_slice_in_dim(wafer_group, mine * count, count)
    my_gains = lax.dynamic_slice_in_dim(gains, mine * count, count)

    out = pl.pallas_call(
        functools.partial(filter_kernel, nt, slabs, cyc, count, half),
        out_shape=jax.ShapeDtypeStruct((HALVES, rows * slabs, 128), F32),
        in_specs=[smem, smem] + [vmem] * 10,
        out_specs=hbm,
        scratch_shapes=[
            pltpu.VMEM((nt, HALVES, count * slabs, 128), F32),
            pltpu.VMEM((CHUNK * half, 2 * QP), F32),
            pltpu.VMEM((CHUNK * half, 2 * QP), F32),
            pltpu.VMEM((nt, HALVES, count * slabs, 128), F32),
            dma((count // CHUNK,)), dma((count // CHUNK, nt)), dma((count // CHUNK, nt)),
        ],
        compiler_params=pltpu.CompilerParams(
            collective_id=1, has_side_effects=True, vmem_limit_bytes=50 * 2**20),
        name="filter",
    )(my_group, my_gains, raw, vraw, by_group, weights, e,
      jnp.asarray(f1), jnp.asarray(tw), jnp.asarray(m2), jnp.asarray(m3), jnp.asarray(f4))
    filtered = pl.pallas_call(
        functools.partial(unpack_kernel, slabs),
        out_shape=jax.ShapeDtypeStruct((rows, samp), F32),
        grid=(rows // BAND,),
        in_specs=[pl.BlockSpec((HALVES, BAND * slabs, 128), lambda i: (0, i, 0))],
        out_specs=pl.BlockSpec((BAND, samp), lambda i: (i, 0)),
        compiler_params=pltpu.CompilerParams(vmem_limit_bytes=32 * 2**20),
        name="unpack",
    )(out)
    return (filtered, gains, template)


def solution(mesh):
    in_specs = (P("det", "tm"), P("det"), P("det", "tm"), P("det"), P())
    out_specs = (P("det", "tm"), P("det"), P(None, "tm"))
    return jax.shard_map(local, mesh=mesh, in_specs=in_specs, out_specs=out_specs, check_vma=False)
```

```python
import functools
import math

import jax
import jax.numpy as jnp
import numpy as np
from jax import lax
from jax.experimental import pallas as pl
from jax.experimental.pallas import tpu as pltpu
from jax.sharding import PartitionSpec as P

ITERS = 3
Q = 250
QP = 256
GP = 16
HALVES = QP // 128
BAND = 32
PIECES = 8
CHUNK = 8
MESH = pl.DeviceIdType.MESH
F32 = jnp.float32
BF16 = jnp.bfloat16
NT_DIMS = (((1,), (1,)), ((), ()))


def dot(a, b):
    return jnp.dot(a, b, preferred_element_type=F32)


def dot_nt(a, b):
    return lax.dot_general(a, b, NT_DIMS, preferred_element_type=F32)


def split(a):
    hi = a.astype(BF16)
    return hi, (a - hi.astype(F32)).astype(BF16)


def np_split(a):
    hi = a.astype(BF16)
    return hi, (a - hi.astype(np.float64)).astype(BF16)


def pack_kernel(slabs, x_ref, out_ref):
    for p in range(slabs):
        wide = x_ref[:, Q * p:Q * (p + 1)]
        wide = jnp.concatenate([wide, jnp.zeros((BAND, QP - Q), F32)], axis=1)
        for h in range(HALVES):
            out_ref[h, pl.ds(p, BAND, stride=slabs), :] = wide[:, 128 * h:128 * (h + 1)]


def unpack_kernel(slabs, y_ref, out_ref):
    for p in range(slabs):
        wide = jnp.concatenate([y_ref[h, pl.ds(p, BAND, stride=slabs), :] for h in range(HALVES)], axis=1)
        out_ref[:, Q * p:Q * (p + 1)] = wide[:, :Q]


def fit_kernel(nd, nt, slabs, own, cyc, rows,
               x_hbm, v_ref, vrc_ref, group_ref, guess_ref, e_ref,
               raw_ref, vraw_ref, tmpl_ref, gains_ref,
               xv, xh, xl, part, small, rbuf, rsmall, tbuf, red,
               loc_sem, raw_s, raw_r, val_s, val_r, ps, pr, ss, sr, ts, tr, gs, gr, fs, fr):
    det = lax.axis_index("det")
    tm = lax.axis_index("tm")
    cycles = slabs // cyc
    share = rows // nt * slabs
    vshare = rows // nt * cycles

    def det_peer(off):
        return lax.rem(det + off, nd)

    def tm_peer(off):
        return lax.rem(tm + off, nt)

    load = pltpu.make_async_copy(x_hbm, xv, loc_sem.at[0])
    load.start()
    barrier = pltpu.get_barrier_semaphore()
    for off in range(1, nd):
        pl.semaphore_signal(barrier, inc=1, device_id=(det_peer(off), tm), device_id_type=MESH)
    for off in range(1, nt):
        pl.semaphore_signal(barrier, inc=1, device_id=(det, tm_peer(off)), device_id_type=MESH)
    pl.semaphore_wait(barrier, nd + nt - 2)

    waits = []
    piece = share // PIECES

    def send_piece(j):
        for off in range(1, nt):
            peer = tm_peer(off)
            copy = pltpu.make_async_remote_copy(
                src_ref=x_hbm.at[:, pl.ds(peer * share + j * piece, piece)],
                dst_ref=raw_ref.at[tm, :, pl.ds(j * piece, piece)],
                send_sem=raw_s.at[j, off], recv_sem=raw_r.at[j, off],
                device_id=(det, peer), device_id_type=MESH)
            copy.start()
            waits.append(copy)

    for off in range(1, nt):
        peer = tm_peer(off)
        copy = pltpu.make_async_remote_copy(
            src_ref=vrc_ref.at[pl.ds(peer * vshare, vshare)], dst_ref=vraw_ref.at[tm],
            send_sem=val_s.at[off], recv_sem=val_r.at[off],
            device_id=(det, peer), device_id_type=MESH)
        copy.start()
        waits.append(copy)
    for j in range(PIECES - 2 * ITERS):
        send_piece(j)
    own_raw = pltpu.make_async_copy(x_hbm.at[:, pl.ds(tm * share, share)], raw_ref.at[tm], loc_sem.at[1])
    own_raw.start()
    own_val = pltpu.make_async_copy(vrc_ref.at[pl.ds(tm * vshare, vshare)], vraw_ref.at[tm], loc_sem.at[2])
    own_val.start()
    load.wait()

    def prepare(i, carry):
        spread = e_ref[i]
        for c in range(cycles):
            slab = c * cyc + i
            mask = dot(v_ref[c], spread)
            x = jnp.concatenate(
                [xv[h, pl.ds(slab, rows, stride=slabs), :] for h in range(HALVES)], axis=1)
            hi, lo = split(mask * x)
            xh[slab] = hi
            xl[slab] = lo
        return carry

    lax.fori_loop(0, cyc, prepare, 0)

    hot = (lax.broadcasted_iota(jnp.int32, (GP, rows), 0) == group_ref[...]).astype(F32)
    lane = lax.broadcasted_iota(jnp.int32, (GP, 128), 1)
    gains = guess_ref[...]
    padded = own * nd
    for it in range(ITERS):
        weight = hot * gains
        wh, wl = split(weight)
        wboth = jnp.concatenate([wh, wl], axis=0)
        power = hot * (gains * gains)
        ph, plo = split(power)
        squares = jnp.sum(power, axis=1, keepdims=True)
        counts = jnp.sum(hot, axis=1, keepdims=True)
        for c in range(cycles):
            block_sum = dot(ph, v_ref[c]) + dot(plo, v_ref[c])
            small[it, c] = jnp.where(lane == 64, squares, jnp.where(lane == 65, counts, block_sum))

        copies = []
        for off in range(1, nd):
            copy = pltpu.make_async_remote_copy(
                src_ref=small.at[it], dst_ref=rsmall.at[it, off],
                send_sem=ss.at[it, off], recv_sem=sr.at[it, off],
                device_id=(det_peer(off), tm), device_id_type=MESH)
            copy.start()
            copies.append(copy)

        def weigh(owner):
            def one(k, carry):
                slab = jnp.minimum(owner * own + k, slabs - 1)
                both = dot(wboth, xh[slab])
                part[it, owner * own + k] = both[:GP] + both[GP:] + dot(wh, xl[slab])
                return carry
            lax.fori_loop(0, own, one, 0, unroll=True)

        for off in range(1, nd):
            peer = det_peer(off)
            weigh(peer)
            copy = pltpu.make_async_remote_copy(
                src_ref=part.at[it, pl.ds(peer * own, own)], dst_ref=rbuf.at[it, off],
                send_sem=ps.at[it, off], recv_sem=pr.at[it, off],
                device_id=(peer, tm), device_id_type=MESH)
            copy.start()
            copies.append(copy)
        send_piece(PIECES - 2 * ITERS + 2 * it)
        weigh(det)
        for copy in copies:
            copy.wait_recv()
        waits_send = copies

        first = small[it]
        for off in range(1, nd):
            first = first + rsmall[it, off]
        scale = jnp.sqrt(first[0][:, 64:65] / jnp.maximum(first[0][:, 65:66], 1.0) + 1e-05)
        small[ITERS] = first
        for k in range(own):
            slab = det * own + k
            total = part[it, slab]
            for off in range(1, nd):
                total = total + rbuf[it, off, k]
            safe = jnp.minimum(slab, slabs - 1)
            sums = small[ITERS, lax.div(safe, cyc)]
            sums = jnp.where(lane < 64, sums, 0.0)
            s1, s2 = split(sums)
            spread = e_ref[lax.rem(safe, cyc)]
            wide = dot(s1, spread) + dot(s2, spread)
            tbuf[it, slab] = (total / scale) / (1.0 + wide / (scale * scale))
        gather = []
        for off in range(1, nd):
            copy = pltpu.make_async_remote_copy(
                src_ref=tbuf.at[it, pl.ds(det * own, own)], dst_ref=tbuf.at[it, pl.ds(det * own, own)],
                send_sem=ts.at[it, off], recv_sem=tr.at[it, off],
                device_id=(det_peer(off), tm), device_id_type=MESH)
            copy.start()
            gather.append(copy)
        send_piece(PIECES - 2 * ITERS + 2 * it + 1)
        for off in range(1, nd):
            source = lax.rem(det + nd - off, nd)
            pltpu.make_async_remote_copy(
                src_ref=tbuf.at[it, pl.ds(source * own, own)], dst_ref=tbuf.at[it, pl.ds(source * own, own)],
                send_sem=ts.at[it, off], recv_sem=tr.at[it, off],
                device_id=(det_peer(off), tm), device_id_type=MESH).wait_recv()
        waits_send = waits_send + gather

        if it == ITERS - 1:
            for off in range(1, nt):
                copy = pltpu.make_async_remote_copy(
                    src_ref=tbuf.at[it, pl.ds(0, slabs)], dst_ref=tmpl_ref.at[tm],
                    send_sem=fs.at[off], recv_sem=fr.at[off],
                    device_id=(det, tm_peer(off)), device_id_type=MESH)
                copy.start()
                waits.append(copy)
            own_tmpl = pltpu.make_async_copy(tbuf.at[it, pl.ds(0, slabs)], tmpl_ref.at[tm], loc_sem.at[3])
            own_tmpl.start()

        def correlate(i, carry):
            inner, blocks = carry
            new_blocks = []
            for c in range(cycles):
                slab = c * cyc + i
                th, tl = split(tbuf[it, slab])
                both = dot_nt(jnp.concatenate([th, tl], axis=0), xh[slab])
                inner = inner + both[:GP] + both[GP:] + dot_nt(th, xl[slab])
                sh, sl = split(tbuf[it, slab] * tbuf[it, slab])
                both = dot_nt(jnp.concatenate([sh, sl], axis=0), e_ref[i])
                new_blocks.append(blocks[c] + both[:GP] + both[GP:])
            return inner, tuple(new_blocks)

        inner, blocks = lax.fori_loop(
            0, cyc, correlate,
            (jnp.zeros((GP, rows), F32), tuple(jnp.zeros((GP, 128), F32) for _ in range(cycles))))
        norm = jnp.zeros((GP, rows), F32)
        for c in range(cycles):
            bh, bl = split(blocks[c])
            norm = norm + dot_nt(bh, v_ref[c]) + dot_nt(bl, v_ref[c])
        numer = jnp.sum(hot * inner, axis=0, keepdims=True)
        denom = jnp.sum(hot * norm, axis=0, keepdims=True)
        red[it, tm] = jnp.concatenate([numer, denom, jnp.zeros((6, rows), F32)], axis=0)
        copies = []
        for off in range(1, nt):
            copy = pltpu.make_async_remote_copy(
                src_ref=red.at[it, tm], dst_ref=red.at[it, tm],
                send_sem=gs.at[it, off], recv_sem=gr.at[it, off],
                device_id=(det, tm_peer(off)), device_id_type=MESH)
            copy.start()
            copies.append(copy)
        for off in range(1, nt):
            source = lax.rem(tm + nt - off, nt)
            pltpu.make_async_remote_copy(
                src_ref=red.at[it, source], dst_ref=red.at[it, source],
                send_sem=gs.at[it, off], recv_sem=gr.at[it, off],
                device_id=(det, tm_peer(off)), device_id_type=MESH).wait_recv()
        total = red[it, 0]
        for t in range(1, nt):
            total = total + red[it, t]
        gains = total[0:1] / (1.0 + total[1:2])
        for copy in waits_send + copies:
            copy.wait_send()

    gains_ref[...] = gains
    own_raw.wait()
    own_val.wait()
    own_tmpl.wait()
    for copy in waits:
        copy.wait()


def filter_kernel(nt, slabs, cyc, count, half,
                  group_ref, gain_ref, raw_ref, v_ref, tmpl_ref, w_ref, e_ref,
                  f1_ref, tw_ref, m2_ref, m3_ref, f4_ref,
                  out_ref, mask, stage, spec, ybuf, loc_sem, send, recv):
    det = lax.axis_index("det")
    tm = lax.axis_index("tm")
    total = slabs * nt
    span = CHUNK * slabs
    chunks = count // CHUNK
    cycles = slabs // cyc

    barrier = pltpu.get_barrier_semaphore()
    for off in range(1, nt):
        pl.semaphore_signal(barrier, inc=1, device_id=(det, lax.rem(tm + off, nt)), device_id_type=MESH)
    pl.semaphore_wait(barrier, nt - 1)

    def spread(i, carry):
        for t in range(nt):
            wide = dot(v_ref[t].astype(BF16), e_ref[i])
            for h in range(HALVES):
                mask[t, h, pl.ds(i, count * cycles, stride=cyc), :] = wide[:, 128 * h:128 * (h + 1)]
        return carry

    lax.fori_loop(0, cyc, spread, 0)

    def remote(chunk, off):
        peer = lax.rem(tm + off, nt)
        return pltpu.make_async_remote_copy(
            src_ref=ybuf.at[peer, :, pl.ds(chunk * span, span)],
            dst_ref=out_ref.at[:, pl.ds((tm * chunks + chunk) * span, span)],
            send_sem=send.at[chunk, off], recv_sem=recv.at[chunk, off],
            device_id=(det, peer), device_id_type=MESH)

    def local(chunk):
        return pltpu.make_async_copy(
            ybuf.at[tm, :, pl.ds(chunk * span, span)],
            out_ref.at[:, pl.ds((tm * chunks + chunk) * span, span)], loc_sem.at[chunk])

    def three(a, b):
        hi, lo = split(a)
        return dot(hi, b[0]) + dot(lo, b[0]) + dot(hi, b[1])

    def rows_of(read, chunk, k):
        if slabs % 8 == 0:
            return read(pl.ds((chunk * CHUNK + k) * slabs, slabs))
        return read(pl.ds(chunk * span, span))[k * slabs:(k + 1) * slabs]

    def work(chunk, carry):
        for k in range(CHUNK):
            row = chunk * CHUNK + k
            g = group_ref[row]
            parts = []
            for t in range(nt):
                seen = jnp.concatenate(
                    [rows_of(lambda at: mask[t, h, at, :], chunk, k) for h in range(HALVES)], axis=1)
                stream = jnp.concatenate(
                    [rows_of(lambda at: raw_ref[t, h, at, :], chunk, k) for h in range(HALVES)], axis=1)
                parts.append(seen * (stream - gain_ref[row] * tmpl_ref[g, pl.ds(t * slabs, slabs), :]))
            x = jnp.concatenate(parts, axis=0)
            hi, lo = split(x)
            both = dot(f1_ref[...], hi)
            y = both[:2 * half] + both[2 * half:] + dot(f1_ref[pl.ds(0, 2 * half), :], lo)
            re, im = y[:half], y[half:]
            stage[pl.ds(k * half, half), pl.ds(0, QP)] = re * tw_ref[0] + im * tw_ref[1]
            stage[pl.ds(k * half, half), pl.ds(QP, QP)] = im * tw_ref[0] - re * tw_ref[1]
        spec[...] = three(stage[...], m2_ref)
        for k in range(CHUNK):
            w = w_ref[group_ref[chunk * CHUNK + k]]
            for h in range(2):
                at = (pl.ds(k * half, half), pl.ds(h * QP, QP))
                spec[at] = spec[at] * w
        stage[...] = three(spec[...], m3_ref)
        held = []
        for k in range(CHUNK):
            row = chunk * CHUNK + k
            re = stage[pl.ds(k * half, half), pl.ds(0, QP)]
            im = stage[pl.ds(k * half, half), pl.ds(QP, QP)]
            v = jnp.concatenate([re * tw_ref[0] - im * tw_ref[1], im * tw_ref[0] + re * tw_ref[1]], axis=0)
            hi, lo = split(v)
            both = dot(f4_ref[...], hi)
            y = both[:total] + both[total:] + dot(f4_ref[pl.ds(0, total), :], lo)
            held.append(y)
            if slabs % 8 == 0:
                for t in range(nt):
                    for h in range(HALVES):
                        ybuf[t, h, pl.ds(row * slabs, slabs), :] = y[t * slabs:(t + 1) * slabs, 128 * h:128 * (h + 1)]
        if slabs % 8:
            for t in range(nt):
                joined = jnp.concatenate([y[t * slabs:(t + 1) * slabs] for y in held], axis=0)
                for h in range(HALVES):
                    ybuf[t, h, pl.ds(chunk * span, span), :] = joined[:, 128 * h:128 * (h + 1)]
        for off in range(1, nt):
            remote(chunk, off).start()
        local(chunk).start()
        return carry

    lax.fori_loop(0, chunks, work, 0)

    def finish(chunk, carry):
        local(chunk).wait()
        for off in range(1, nt):
            remote(chunk, off).wait_send()
        for off in range(1, nt):
            source = lax.rem(tm + nt - off, nt)
            pltpu.make_async_remote_copy(
                src_ref=ybuf.at[source, :, pl.ds(chunk * span, span)],
                dst_ref=out_ref.at[:, pl.ds((source * chunks + chunk) * span, span)],
                send_sem=send.at[chunk, off], recv_sem=recv.at[chunk, off],
                device_id=(det, source), device_id_type=MESH).wait_recv()
        return carry

    lax.fori_loop(0, chunks, finish, 0)


def constants(total):
    length = total * Q
    half = -(-(total // 2 + 1) // 8) * 8
    kp = np.arange(total // 2 + 1)
    n = kp.size
    p = np.arange(total)
    angle = 2 * np.pi / total * (kp[:, None] * p[None, :] % total)
    f1 = np.zeros((2 * half, total))
    f1[:n] = np.cos(angle)
    f1[half:half + n] = -np.sin(angle)
    hi, lo = np_split(f1)
    f1 = np.concatenate([hi, lo], axis=0)
    twice = np.where((kp == 0) | (2 * kp == total), 1.0, 2.0) / length
    f4 = np.zeros((total, 2 * half))
    f4[:, :n] = (np.cos(angle) * twice[:, None]).T
    f4[:, half:half + n] = -(np.sin(angle) * twice[:, None]).T
    hi, lo = np_split(f4)
    f4 = np.concatenate([hi, lo], axis=0)
    q = np.arange(Q)
    angle = 2 * np.pi / length * (kp[:, None] * q[None, :])
    tw = np.zeros((2, half, QP), np.float32)
    tw[0, :n, :Q] = np.cos(angle)
    tw[1, :n, :Q] = np.sin(angle)
    angle = 2 * np.pi / Q * (q[:, None] * q[None, :] % Q)
    c, s = np.cos(angle), np.sin(angle)

    def complex_table(sign):
        m = np.zeros((2 * QP, 2 * QP))
        m[:Q, :Q] = c
        m[QP:QP + Q, :Q] = -sign * s
        m[:Q, QP:QP + Q] = sign * s
        m[QP:QP + Q, QP:QP + Q] = c
        return np.stack(np_split(m))

    return half, n, f1, f4, tw, complex_table(-1.0), complex_table(1.0)


def local(timestreams, wafer_group, valid_blocks, gain_guess, inverse_psd):
    nd, nt = lax.axis_size("det"), lax.axis_size("tm")
    rows, samp = timestreams.shape
    groups = inverse_psd.shape[0]
    block = samp // valid_blocks.shape[1]
    cyc = block // math.gcd(block, Q)
    per = cyc * Q // block
    slabs = samp // Q
    cycles = slabs // cyc
    own = -(-slabs // nd)
    padded = own * nd
    count = rows // nt
    total = slabs * nt
    half, n, f1, f4, tw, m2, m3 = constants(total)
    spread = np.zeros((cyc, 128, QP), np.float32)
    for i in range(cyc):
        spread[i, (i * Q + np.arange(Q)) // block, np.arange(Q)] = 1.0
    e = jnp.asarray(spread.astype(BF16))

    x2 = pl.pallas_call(
        functools.partial(pack_kernel, slabs),
        out_shape=jax.ShapeDtypeStruct((HALVES, rows * slabs, 128), F32),
        grid=(rows // BAND,),
        in_specs=[pl.BlockSpec((BAND, samp), lambda i: (i, 0))],
        out_specs=pl.BlockSpec((HALVES, BAND * slabs, 128), lambda i: (0, i, 0)),
        compiler_params=pltpu.CompilerParams(vmem_limit_bytes=32 * 2**20),
        name="pack",
    )(timestreams)
    vrc = jnp.pad(valid_blocks.astype(F32).reshape(rows, cycles, per), ((0, 0), (0, 0), (0, 128 - per)))
    v = jnp.transpose(vrc, (1, 0, 2)).astype(BF16)
    vrc = vrc.reshape(rows * cycles, 128)

    vmem = pl.BlockSpec(memory_space=pltpu.VMEM)
    hbm = pl.BlockSpec(memory_space=pl.ANY)
    smem = pl.BlockSpec(memory_space=pltpu.SMEM)
    dma = pltpu.SemaphoreType.DMA
    raw, vraw, tmpl, gains = pl.pallas_call(
        functools.partial(fit_kernel, nd, nt, slabs, own, cyc, rows),
        out_shape=(
            jax.ShapeDtypeStruct((nt, HALVES, count * slabs, 128), F32),
            jax.ShapeDtypeStruct((nt, count * cycles, 128), F32),
            jax.ShapeDtypeStruct((nt, slabs, GP, QP), F32),
            jax.ShapeDtypeStruct((1, rows), F32),
        ),
        in_specs=[hbm, vmem, vmem, vmem, vmem, vmem],
        out_specs=(hbm, vmem, hbm, vmem),
        scratch_shapes=[
            pltpu.VMEM((HALVES, rows * slabs, 128), F32),
            pltpu.VMEM((slabs, rows, QP), BF16),
            pltpu.VMEM((slabs, rows, QP), BF16),
            pltpu.VMEM((ITERS, padded, GP, QP), F32),
            pltpu.VMEM((ITERS + 1, cycles, GP, 128), F32),
            pltpu.VMEM((ITERS, nd, own, GP, QP), F32),
            pltpu.VMEM((ITERS, nd, cycles, GP, 128), F32),
            pltpu.VMEM((ITERS, padded, GP, QP), F32),
            pltpu.VMEM((ITERS, nt, 8, rows), F32),
            dma((4,)), dma((PIECES, nt)), dma((PIECES, nt)), dma((nt,)), dma((nt,)),
            dma((ITERS, nd)), dma((ITERS, nd)), dma((ITERS, nd)), dma((ITERS, nd)),
            dma((ITERS, nd)), dma((ITERS, nd)), dma((ITERS, nt)), dma((ITERS, nt)),
            dma((nt,)), dma((nt,)),
        ],
        compiler_params=pltpu.CompilerParams(
            collective_id=0, has_side_effects=True, vmem_limit_bytes=50 * 2**20),
        name="fit",
    )(x2, v, vrc, wafer_group.reshape(1, rows), gain_guess.reshape(1, rows), e)

    gains = gains.reshape(rows)
    mine = lax.axis_index("tm")
    template = lax.dynamic_index_in_dim(tmpl, mine, 0, False)[:, :groups, :Q]
    template = jnp.transpose(template, (1, 0, 2)).reshape(groups, samp)
    by_group = jnp.transpose(tmpl.reshape(total, GP, QP), (1, 0, 2))[:groups]
    kp = np.arange(n)
    pick = np.zeros((total, 2 * half), np.float32)
    pick[kp, kp] = 0.5
    pick[(total - kp) % total, half + kp] = 0.5
    both = jnp.einsum("gjp,pk->gkj", inverse_psd.reshape(groups, Q, total), pick, precision=lax.Precision.HIGHEST)
    flips = np.zeros((2, Q, QP), np.float32)
    flips[0, (Q - np.arange(Q)) % Q, np.arange(Q)] = 1.0
    flips[1, Q - 1 - np.arange(Q), np.arange(Q)] = 1.0
    edge = jnp.dot(both[:, half], flips[0], precision=lax.Precision.HIGHEST)
    inside = jnp.einsum("gkj,jq->gkq", both[:, half + 1:], flips[1], precision=lax.Precision.HIGHEST)
    weights = jnp.pad(both[:, :half], ((0, 0), (0, 0), (0, QP - Q))) + jnp.concatenate([edge[:, None], inside], axis=1)
    my_group = lax.dynamic_slice_in_dim(wafer_group, mine * count, count)
    my_gains = lax.dynamic_slice_in_dim(gains, mine * count, count)

    out = pl.pallas_call(
        functools.partial(filter_kernel, nt, slabs, cyc, count, half),
        out_shape=jax.ShapeDtypeStruct((HALVES, rows * slabs, 128), F32),
        in_specs=[smem, smem] + [vmem] * 10,
        out_specs=hbm,
        scratch_shapes=[
            pltpu.VMEM((nt, HALVES, count * slabs, 128), F32),
            pltpu.VMEM((CHUNK * half, 2 * QP), F32),
            pltpu.VMEM((CHUNK * half, 2 * QP), F32),
            pltpu.VMEM((nt, HALVES, count * slabs, 128), F32),
            dma((count // CHUNK,)), dma((count // CHUNK, nt)), dma((count // CHUNK, nt)),
        ],
        compiler_params=pltpu.CompilerParams(
            collective_id=1, has_side_effects=True, vmem_limit_bytes=50 * 2**20),
        name="filter",
    )(my_group, my_gains, raw, vraw, by_group, weights, e,
      jnp.asarray(f1), jnp.asarray(tw), jnp.asarray(m2), jnp.asarray(m3), jnp.asarray(f4))
    filtered = pl.pallas_call(
        functools.partial(unpack_kernel, slabs),
        out_shape=jax.ShapeDtypeStruct((rows, samp), F32),
        grid=(rows // BAND,),
        in_specs=[pl.BlockSpec((HALVES, BAND * slabs, 128), lambda i: (0, i, 0))],
        out_specs=pl.BlockSpec((BAND, samp), lambda i: (i, 0)),
        compiler_params=pltpu.CompilerParams(vmem_limit_bytes=32 * 2**20),
        name="unpack",
    )(out)
    return (filtered, gains, template)


def solution(mesh):
    in_specs = (P("det", "tm"), P("det"), P("det", "tm"), P("det"), P())
    out_specs = (P("det", "tm"), P("det"), P(None, "tm"))
    return jax.shard_map(local, mesh=mesh, in_specs=in_specs, out_specs=out_specs, check_vma=False)
```

```python
import functools
import math

import jax
import jax.numpy as jnp
import numpy as np
from jax import lax
from jax.experimental import pallas as pl
from jax.experimental.pallas import tpu as pltpu
from jax.sharding import PartitionSpec as P

ITERS = 3
Q = 250
QP = 256
GP = 16
HALVES = QP // 128
BAND = 128
PIECES = 8
CHUNK = 8
MESH = pl.DeviceIdType.MESH
F32 = jnp.float32
BF16 = jnp.bfloat16
NT_DIMS = (((1,), (1,)), ((), ()))


def dot(a, b):
    return jnp.dot(a, b, preferred_element_type=F32)


def dot_nt(a, b):
    return lax.dot_general(a, b, NT_DIMS, preferred_element_type=F32)


def split(a):
    hi = a.astype(BF16)
    return hi, (a - hi.astype(F32)).astype(BF16)


def np_split(a):
    hi = a.astype(BF16)
    return hi, (a - hi.astype(np.float64)).astype(BF16)


def pack_kernel(slabs, x_ref, out_ref):
    for p in range(slabs):
        tall = jnp.concatenate([x_ref[Q * p:Q * (p + 1), :], jnp.zeros((QP - Q, BAND), F32)], axis=0)
        for h in range(HALVES):
            out_ref[h, pl.ds(p, BAND, stride=slabs), :] = tall[128 * h:128 * (h + 1)].T


def unpack_kernel(slabs, y_ref, out_ref):
    for p in range(slabs):
        tall = jnp.concatenate([y_ref[h, pl.ds(p, BAND, stride=slabs), :].T for h in range(HALVES)], axis=0)
        out_ref[Q * p:Q * (p + 1), :] = tall[:Q]


def fit_kernel(nd, nt, slabs, own, cyc, rows,
               x_hbm, v_ref, vrc_ref, group_ref, guess_ref, e_ref,
               raw_ref, vraw_ref, tmpl_ref, gains_ref,
               xv, xh, xl, part, small, rbuf, rsmall, tbuf, red,
               loc_sem, raw_s, raw_r, val_s, val_r, ps, pr, ss, sr, ts, tr, gs, gr, fs, fr):
    det = lax.axis_index("det")
    tm = lax.axis_index("tm")
    cycles = slabs // cyc
    share = rows // nt * slabs
    vshare = rows // nt * cycles

    def det_peer(off):
        return lax.rem(det + off, nd)

    def tm_peer(off):
        return lax.rem(tm + off, nt)

    load = pltpu.make_async_copy(x_hbm, xv, loc_sem.at[0])
    load.start()
    barrier = pltpu.get_barrier_semaphore()
    for off in range(1, nd):
        pl.semaphore_signal(barrier, inc=1, device_id=(det_peer(off), tm), device_id_type=MESH)
    for off in range(1, nt):
        pl.semaphore_signal(barrier, inc=1, device_id=(det, tm_peer(off)), device_id_type=MESH)
    pl.semaphore_wait(barrier, nd + nt - 2)

    waits = []
    piece = share // PIECES

    def send_piece(j):
        for off in range(1, nt):
            peer = tm_peer(off)
            copy = pltpu.make_async_remote_copy(
                src_ref=x_hbm.at[:, pl.ds(peer * share + j * piece, piece)],
                dst_ref=raw_ref.at[tm, :, pl.ds(j * piece, piece)],
                send_sem=raw_s.at[j, off], recv_sem=raw_r.at[j, off],
                device_id=(det, peer), device_id_type=MESH)
            copy.start()
            waits.append(copy)

    for off in range(1, nt):
        peer = tm_peer(off)
        copy = pltpu.make_async_remote_copy(
            src_ref=vrc_ref.at[pl.ds(peer * vshare, vshare)], dst_ref=vraw_ref.at[tm],
            send_sem=val_s.at[off], recv_sem=val_r.at[off],
            device_id=(det, peer), device_id_type=MESH)
        copy.start()
        waits.append(copy)
    for j in range(PIECES - 2 * ITERS):
        send_piece(j)
    own_raw = pltpu.make_async_copy(x_hbm.at[:, pl.ds(tm * share, share)], raw_ref.at[tm], loc_sem.at[1])
    own_raw.start()
    own_val = pltpu.make_async_copy(vrc_ref.at[pl.ds(tm * vshare, vshare)], vraw_ref.at[tm], loc_sem.at[2])
    own_val.start()
    load.wait()

    def prepare(i, carry):
        spread = e_ref[i]
        for c in range(cycles):
            slab = c * cyc + i
            mask = dot(v_ref[c], spread)
            x = jnp.concatenate(
                [xv[h, pl.ds(slab, rows, stride=slabs), :] for h in range(HALVES)], axis=1)
            hi, lo = split(mask * x)
            xh[slab] = hi
            xl[slab] = lo
        return carry

    lax.fori_loop(0, cyc, prepare, 0)

    hot = (lax.broadcasted_iota(jnp.int32, (GP, rows), 0) == group_ref[...]).astype(F32)
    lane = lax.broadcasted_iota(jnp.int32, (GP, 128), 1)
    gains = guess_ref[...]
    padded = own * nd
    for it in range(ITERS):
        weight = hot * gains
        wh, wl = split(weight)
        wboth = jnp.concatenate([wh, wl], axis=0)
        power = hot * (gains * gains)
        ph, plo = split(power)
        squares = jnp.sum(power, axis=1, keepdims=True)
        counts = jnp.sum(hot, axis=1, keepdims=True)
        for c in range(cycles):
            block_sum = dot(ph, v_ref[c]) + dot(plo, v_ref[c])
            small[it, c] = jnp.where(lane == 64, squares, jnp.where(lane == 65, counts, block_sum))

        copies = []
        for off in range(1, nd):
            copy = pltpu.make_async_remote_copy(
                src_ref=small.at[it], dst_ref=rsmall.at[it, off],
                send_sem=ss.at[it, off], recv_sem=sr.at[it, off],
                device_id=(det_peer(off), tm), device_id_type=MESH)
            copy.start()
            copies.append(copy)

        def weigh(owner):
            def one(k, carry):
                slab = jnp.minimum(owner * own + k, slabs - 1)
                both = dot(wboth, xh[slab])
                part[it, owner * own + k] = both[:GP] + both[GP:] + dot(wh, xl[slab])
                return carry
            lax.fori_loop(0, own, one, 0, unroll=True)

        for off in range(1, nd):
            peer = det_peer(off)
            weigh(peer)
            copy = pltpu.make_async_remote_copy(
                src_ref=part.at[it, pl.ds(peer * own, own)], dst_ref=rbuf.at[it, off],
                send_sem=ps.at[it, off], recv_sem=pr.at[it, off],
                device_id=(peer, tm), device_id_type=MESH)
            copy.start()
            copies.append(copy)
        send_piece(PIECES - 2 * ITERS + 2 * it)
        weigh(det)
        for copy in copies:
            copy.wait_recv()
        waits_send = copies

        first = small[it]
        for off in range(1, nd):
            first = first + rsmall[it, off]
        scale = jnp.sqrt(first[0][:, 64:65] / jnp.maximum(first[0][:, 65:66], 1.0) + 1e-05)
        small[ITERS] = first
        for k in range(own):
            slab = det * own + k
            total = part[it, slab]
            for off in range(1, nd):
                total = total + rbuf[it, off, k]
            safe = jnp.minimum(slab, slabs - 1)
            sums = small[ITERS, lax.div(safe, cyc)]
            sums = jnp.where(lane < 64, sums, 0.0)
            s1, s2 = split(sums)
            spread = e_ref[lax.rem(safe, cyc)]
            wide = dot(s1, spread) + dot(s2, spread)
            tbuf[it, slab] = (total / scale) / (1.0 + wide / (scale * scale))
        gather = []
        for off in range(1, nd):
            copy = pltpu.make_async_remote_copy(
                src_ref=tbuf.at[it, pl.ds(det * own, own)], dst_ref=tbuf.at[it, pl.ds(det * own, own)],
                send_sem=ts.at[it, off], recv_sem=tr.at[it, off],
                device_id=(det_peer(off), tm), device_id_type=MESH)
            copy.start()
            gather.append(copy)
        send_piece(PIECES - 2 * ITERS + 2 * it + 1)
        for off in range(1, nd):
            source = lax.rem(det + nd - off, nd)
            pltpu.make_async_remote_copy(
                src_ref=tbuf.at[it, pl.ds(source * own, own)], dst_ref=tbuf.at[it, pl.ds(source * own, own)],
                send_sem=ts.at[it, off], recv_sem=tr.at[it, off],
                device_id=(det_peer(off), tm), device_id_type=MESH).wait_recv()
        waits_send = waits_send + gather

        if it == ITERS - 1:
            for off in range(1, nt):
                copy = pltpu.make_async_remote_copy(
                    src_ref=tbuf.at[it, pl.ds(0, slabs)], dst_ref=tmpl_ref.at[tm],
                    send_sem=fs.at[off], recv_sem=fr.at[off],
                    device_id=(det, tm_peer(off)), device_id_type=MESH)
                copy.start()
                waits.append(copy)
            own_tmpl = pltpu.make_async_copy(tbuf.at[it, pl.ds(0, slabs)], tmpl_ref.at[tm], loc_sem.at[3])
            own_tmpl.start()

        def correlate(i, carry):
            inner, blocks = carry
            new_blocks = []
            for c in range(cycles):
                slab = c * cyc + i
                th, tl = split(tbuf[it, slab])
                both = dot_nt(jnp.concatenate([th, tl], axis=0), xh[slab])
                inner = inner + both[:GP] + both[GP:] + dot_nt(th, xl[slab])
                sh, sl = split(tbuf[it, slab] * tbuf[it, slab])
                both = dot_nt(jnp.concatenate([sh, sl], axis=0), e_ref[i])
                new_blocks.append(blocks[c] + both[:GP] + both[GP:])
            return inner, tuple(new_blocks)

        inner, blocks = lax.fori_loop(
            0, cyc, correlate,
            (jnp.zeros((GP, rows), F32), tuple(jnp.zeros((GP, 128), F32) for _ in range(cycles))))
        norm = jnp.zeros((GP, rows), F32)
        for c in range(cycles):
            bh, bl = split(blocks[c])
            norm = norm + dot_nt(bh, v_ref[c]) + dot_nt(bl, v_ref[c])
        numer = jnp.sum(hot * inner, axis=0, keepdims=True)
        denom = jnp.sum(hot * norm, axis=0, keepdims=True)
        red[it, tm] = jnp.concatenate([numer, denom, jnp.zeros((6, rows), F32)], axis=0)
        copies = []
        for off in range(1, nt):
            copy = pltpu.make_async_remote_copy(
                src_ref=red.at[it, tm], dst_ref=red.at[it, tm],
                send_sem=gs.at[it, off], recv_sem=gr.at[it, off],
                device_id=(det, tm_peer(off)), device_id_type=MESH)
            copy.start()
            copies.append(copy)
        for off in range(1, nt):
            source = lax.rem(tm + nt - off, nt)
            pltpu.make_async_remote_copy(
                src_ref=red.at[it, source], dst_ref=red.at[it, source],
                send_sem=gs.at[it, off], recv_sem=gr.at[it, off],
                device_id=(det, tm_peer(off)), device_id_type=MESH).wait_recv()
        total = red[it, 0]
        for t in range(1, nt):
            total = total + red[it, t]
        gains = total[0:1] / (1.0 + total[1:2])
        for copy in waits_send + copies:
            copy.wait_send()

    gains_ref[...] = gains
    own_raw.wait()
    own_val.wait()
    own_tmpl.wait()
    for copy in waits:
        copy.wait()


def filter_kernel(nt, slabs, cyc, count, half,
                  group_ref, gain_ref, raw_ref, v_ref, tmpl_ref, w_ref, e_ref,
                  f1_ref, tw_ref, m2_ref, m3_ref, f4_ref,
                  out_ref, mask, stage, spec, ybuf, loc_sem, send, recv):
    det = lax.axis_index("det")
    tm = lax.axis_index("tm")
    total = slabs * nt
    span = CHUNK * slabs
    chunks = count // CHUNK
    cycles = slabs // cyc

    barrier = pltpu.get_barrier_semaphore()
    for off in range(1, nt):
        pl.semaphore_signal(barrier, inc=1, device_id=(det, lax.rem(tm + off, nt)), device_id_type=MESH)
    pl.semaphore_wait(barrier, nt - 1)

    def spread(i, carry):
        for t in range(nt):
            wide = dot(v_ref[t].astype(BF16), e_ref[i])
            for h in range(HALVES):
                mask[t, h, pl.ds(i, count * cycles, stride=cyc), :] = wide[:, 128 * h:128 * (h + 1)]
        return carry

    lax.fori_loop(0, cyc, spread, 0)

    def remote(chunk, off):
        peer = lax.rem(tm + off, nt)
        return pltpu.make_async_remote_copy(
            src_ref=ybuf.at[peer, :, pl.ds(chunk * span, span)],
            dst_ref=out_ref.at[:, pl.ds((tm * chunks + chunk) * span, span)],
            send_sem=send.at[chunk, off], recv_sem=recv.at[chunk, off],
            device_id=(det, peer), device_id_type=MESH)

    def local(chunk):
        return pltpu.make_async_copy(
            ybuf.at[tm, :, pl.ds(chunk * span, span)],
            out_ref.at[:, pl.ds((tm * chunks + chunk) * span, span)], loc_sem.at[chunk])

    def three(a, b):
        hi, lo = split(a)
        return dot(hi, b[0]) + dot(lo, b[0]) + dot(hi, b[1])

    def rows_of(read, chunk, k):
        if slabs % 8 == 0:
            return read(pl.ds((chunk * CHUNK + k) * slabs, slabs))
        return read(pl.ds(chunk * span, span))[k * slabs:(k + 1) * slabs]

    def work(chunk, carry):
        for k in range(CHUNK):
            row = chunk * CHUNK + k
            g = group_ref[row]
            parts = []
            for t in range(nt):
                seen = jnp.concatenate(
                    [rows_of(lambda at: mask[t, h, at, :], chunk, k) for h in range(HALVES)], axis=1)
                stream = jnp.concatenate(
                    [rows_of(lambda at: raw_ref[t, h, at, :], chunk, k) for h in range(HALVES)], axis=1)
                parts.append(seen * (stream - gain_ref[row] * tmpl_ref[g, pl.ds(t * slabs, slabs), :]))
            x = jnp.concatenate(parts, axis=0)
            hi, lo = split(x)
            both = dot(f1_ref[...], hi)
            y = both[:2 * half] + both[2 * half:] + dot(f1_ref[pl.ds(0, 2 * half), :], lo)
            re, im = y[:half], y[half:]
            stage[pl.ds(k * half, half), pl.ds(0, QP)] = re * tw_ref[0] + im * tw_ref[1]
            stage[pl.ds(k * half, half), pl.ds(QP, QP)] = im * tw_ref[0] - re * tw_ref[1]
        spec[...] = three(stage[...], m2_ref)
        for k in range(CHUNK):
            w = w_ref[group_ref[chunk * CHUNK + k]]
            for h in range(2):
                at = (pl.ds(k * half, half), pl.ds(h * QP, QP))
                spec[at] = spec[at] * w
        stage[...] = three(spec[...], m3_ref)
        held = []
        for k in range(CHUNK):
            row = chunk * CHUNK + k
            re = stage[pl.ds(k * half, half), pl.ds(0, QP)]
            im = stage[pl.ds(k * half, half), pl.ds(QP, QP)]
            v = jnp.concatenate([re * tw_ref[0] - im * tw_ref[1], im * tw_ref[0] + re * tw_ref[1]], axis=0)
            hi, lo = split(v)
            both = dot(f4_ref[...], hi)
            y = both[:total] + both[total:] + dot(f4_ref[pl.ds(0, total), :], lo)
            held.append(y)
            if slabs % 8 == 0:
                for t in range(nt):
                    for h in range(HALVES):
                        ybuf[t, h, pl.ds(row * slabs, slabs), :] = y[t * slabs:(t + 1) * slabs, 128 * h:128 * (h + 1)]
        if slabs % 8:
            for t in range(nt):
                joined = jnp.concatenate([y[t * slabs:(t + 1) * slabs] for y in held], axis=0)
                for h in range(HALVES):
                    ybuf[t, h, pl.ds(chunk * span, span), :] = joined[:, 128 * h:128 * (h + 1)]
        for off in range(1, nt):
            remote(chunk, off).start()
        local(chunk).start()
        return carry

    lax.fori_loop(0, chunks, work, 0)

    def finish(chunk, carry):
        local(chunk).wait()
        for off in range(1, nt):
            remote(chunk, off).wait_send()
        for off in range(1, nt):
            source = lax.rem(tm + nt - off, nt)
            pltpu.make_async_remote_copy(
                src_ref=ybuf.at[source, :, pl.ds(chunk * span, span)],
                dst_ref=out_ref.at[:, pl.ds((source * chunks + chunk) * span, span)],
                send_sem=send.at[chunk, off], recv_sem=recv.at[chunk, off],
                device_id=(det, source), device_id_type=MESH).wait_recv()
        return carry

    lax.fori_loop(0, chunks, finish, 0)


def constants(total):
    length = total * Q
    half = -(-(total // 2 + 1) // 8) * 8
    kp = np.arange(total // 2 + 1)
    n = kp.size
    p = np.arange(total)
    angle = 2 * np.pi / total * (kp[:, None] * p[None, :] % total)
    f1 = np.zeros((2 * half, total))
    f1[:n] = np.cos(angle)
    f1[half:half + n] = -np.sin(angle)
    hi, lo = np_split(f1)
    f1 = np.concatenate([hi, lo], axis=0)
    twice = np.where((kp == 0) | (2 * kp == total), 1.0, 2.0) / length
    f4 = np.zeros((total, 2 * half))
    f4[:, :n] = (np.cos(angle) * twice[:, None]).T
    f4[:, half:half + n] = -(np.sin(angle) * twice[:, None]).T
    hi, lo = np_split(f4)
    f4 = np.concatenate([hi, lo], axis=0)
    q = np.arange(Q)
    angle = 2 * np.pi / length * (kp[:, None] * q[None, :])
    tw = np.zeros((2, half, QP), np.float32)
    tw[0, :n, :Q] = np.cos(angle)
    tw[1, :n, :Q] = np.sin(angle)
    angle = 2 * np.pi / Q * (q[:, None] * q[None, :] % Q)
    c, s = np.cos(angle), np.sin(angle)

    def complex_table(sign):
        m = np.zeros((2 * QP, 2 * QP))
        m[:Q, :Q] = c
        m[QP:QP + Q, :Q] = -sign * s
        m[:Q, QP:QP + Q] = sign * s
        m[QP:QP + Q, QP:QP + Q] = c
        return np.stack(np_split(m))

    return half, n, f1, f4, tw, complex_table(-1.0), complex_table(1.0)


def local(timestreams, wafer_group, valid_blocks, gain_guess, inverse_psd):
    nd, nt = lax.axis_size("det"), lax.axis_size("tm")
    rows, samp = timestreams.shape
    groups = inverse_psd.shape[0]
    block = samp // valid_blocks.shape[1]
    cyc = block // math.gcd(block, Q)
    per = cyc * Q // block
    slabs = samp // Q
    cycles = slabs // cyc
    own = -(-slabs // nd)
    padded = own * nd
    count = rows // nt
    total = slabs * nt
    half, n, f1, f4, tw, m2, m3 = constants(total)
    spread = np.zeros((cyc, 128, QP), np.float32)
    for i in range(cyc):
        spread[i, (i * Q + np.arange(Q)) // block, np.arange(Q)] = 1.0
    e = jnp.asarray(spread.astype(BF16))

    x2 = pl.pallas_call(
        functools.partial(pack_kernel, slabs),
        out_shape=jax.ShapeDtypeStruct((HALVES, rows * slabs, 128), F32),
        grid=(rows // BAND,),
        in_specs=[pl.BlockSpec((samp, BAND), lambda i: (0, i))],
        out_specs=pl.BlockSpec((HALVES, BAND * slabs, 128), lambda i: (0, i, 0)),
        compiler_params=pltpu.CompilerParams(vmem_limit_bytes=32 * 2**20),
        name="pack",
    )(timestreams.T)
    vrc = jnp.pad(valid_blocks.astype(F32).reshape(rows, cycles, per), ((0, 0), (0, 0), (0, 128 - per)))
    v = jnp.transpose(vrc, (1, 0, 2)).astype(BF16)
    vrc = vrc.reshape(rows * cycles, 128)

    vmem = pl.BlockSpec(memory_space=pltpu.VMEM)
    hbm = pl.BlockSpec(memory_space=pl.ANY)
    smem = pl.BlockSpec(memory_space=pltpu.SMEM)
    dma = pltpu.SemaphoreType.DMA
    raw, vraw, tmpl, gains = pl.pallas_call(
        functools.partial(fit_kernel, nd, nt, slabs, own, cyc, rows),
        out_shape=(
            jax.ShapeDtypeStruct((nt, HALVES, count * slabs, 128), F32),
            jax.ShapeDtypeStruct((nt, count * cycles, 128), F32),
            jax.ShapeDtypeStruct((nt, slabs, GP, QP), F32),
            jax.ShapeDtypeStruct((1, rows), F32),
        ),
        in_specs=[hbm, vmem, vmem, vmem, vmem, vmem],
        out_specs=(hbm, vmem, hbm, vmem),
        scratch_shapes=[
            pltpu.VMEM((HALVES, rows * slabs, 128), F32),
            pltpu.VMEM((slabs, rows, QP), BF16),
            pltpu.VMEM((slabs, rows, QP), BF16),
            pltpu.VMEM((ITERS, padded, GP, QP), F32),
            pltpu.VMEM((ITERS + 1, cycles, GP, 128), F32),
            pltpu.VMEM((ITERS, nd, own, GP, QP), F32),
            pltpu.VMEM((ITERS, nd, cycles, GP, 128), F32),
            pltpu.VMEM((ITERS, padded, GP, QP), F32),
            pltpu.VMEM((ITERS, nt, 8, rows), F32),
            dma((4,)), dma((PIECES, nt)), dma((PIECES, nt)), dma((nt,)), dma((nt,)),
            dma((ITERS, nd)), dma((ITERS, nd)), dma((ITERS, nd)), dma((ITERS, nd)),
            dma((ITERS, nd)), dma((ITERS, nd)), dma((ITERS, nt)), dma((ITERS, nt)),
            dma((nt,)), dma((nt,)),
        ],
        compiler_params=pltpu.CompilerParams(
            collective_id=0, has_side_effects=True, vmem_limit_bytes=50 * 2**20),
        name="fit",
    )(x2, v, vrc, wafer_group.reshape(1, rows), gain_guess.reshape(1, rows), e)

    gains = gains.reshape(rows)
    mine = lax.axis_index("tm")
    template = lax.dynamic_index_in_dim(tmpl, mine, 0, False)[:, :groups, :Q]
    template = jnp.transpose(template, (1, 0, 2)).reshape(groups, samp)
    by_group = jnp.transpose(tmpl.reshape(total, GP, QP), (1, 0, 2))[:groups]
    kp = np.arange(n)
    pick = np.zeros((total, 2 * half), np.float32)
    pick[kp, kp] = 0.5
    pick[(total - kp) % total, half + kp] = 0.5
    both = jnp.einsum("gjp,pk->gkj", inverse_psd.reshape(groups, Q, total), pick, precision=lax.Precision.HIGHEST)
    flips = np.zeros((2, Q, QP), np.float32)
    flips[0, (Q - np.arange(Q)) % Q, np.arange(Q)] = 1.0
    flips[1, Q - 1 - np.arange(Q), np.arange(Q)] = 1.0
    edge = jnp.dot(both[:, half], flips[0], precision=lax.Precision.HIGHEST)
    inside = jnp.einsum("gkj,jq->gkq", both[:, half + 1:], flips[1], precision=lax.Precision.HIGHEST)
    weights = jnp.pad(both[:, :half], ((0, 0), (0, 0), (0, QP - Q))) + jnp.concatenate([edge[:, None], inside], axis=1)
    my_group = lax.dynamic_slice_in_dim(wafer_group, mine * count, count)
    my_gains = lax.dynamic_slice_in_dim(gains, mine * count, count)

    out = pl.pallas_call(
        functools.partial(filter_kernel, nt, slabs, cyc, count, half),
        out_shape=jax.ShapeDtypeStruct((HALVES, rows * slabs, 128), F32),
        in_specs=[smem, smem] + [vmem] * 10,
        out_specs=hbm,
        scratch_shapes=[
            pltpu.VMEM((nt, HALVES, count * slabs, 128), F32),
            pltpu.VMEM((CHUNK * half, 2 * QP), F32),
            pltpu.VMEM((CHUNK * half, 2 * QP), F32),
            pltpu.VMEM((nt, HALVES, count * slabs, 128), F32),
            dma((count // CHUNK,)), dma((count // CHUNK, nt)), dma((count // CHUNK, nt)),
        ],
        compiler_params=pltpu.CompilerParams(
            collective_id=1, has_side_effects=True, vmem_limit_bytes=50 * 2**20),
        name="filter",
    )(my_group, my_gains, raw, vraw, by_group, weights, e,
      jnp.asarray(f1), jnp.asarray(tw), jnp.asarray(m2), jnp.asarray(m3), jnp.asarray(f4))
    filtered = pl.pallas_call(
        functools.partial(unpack_kernel, slabs),
        out_shape=jax.ShapeDtypeStruct((samp, rows), F32),
        grid=(rows // BAND,),
        in_specs=[pl.BlockSpec((HALVES, BAND * slabs, 128), lambda i: (0, i, 0))],
        out_specs=pl.BlockSpec((samp, BAND), lambda i: (0, i)),
        compiler_params=pltpu.CompilerParams(vmem_limit_bytes=32 * 2**20),
        name="unpack",
    )(out).T
    return (filtered, gains, template)


def solution(mesh):
    in_specs = (P("det", "tm"), P("det"), P("det", "tm"), P("det"), P())
    out_specs = (P("det", "tm"), P("det"), P(None, "tm"))
    return jax.shard_map(local, mesh=mesh, in_specs=in_specs, out_specs=out_specs, check_vma=False)
```
